32 devices in a mesh: groups: 2 (over x), tm: 16 (over z, y, core).
Axes of the slice: x: 2, y: 2, z: 4, core: 2. Of those that a mesh axis runs over, the one named last changes fastest.
Arguments:
- signal: float32 [64, 16384], P(None, ('groups', 'tm')), parts along dimension 1, may hold values from -32 to 32
- dictionary: bfloat16 [256, 64, 128], replicated, may hold values from -4 to 4
- step: float32 [1], replicated, may hold values from 0.04 to 0.08
Outputs:
- codes: float32 [256, 16384], P(None, ('groups', 'tm')), parts along dimension 1
- new_dictionary: float32 [512, 64, 128], P(('groups', 'tm')), parts along dimension 0
- loss: float32 [2], P('groups'), parts along dimension 0
The draws below stay inside these ranges and needn't reach their ends.
There are 2 independent parts, one for each index of `groups`. The reference program is written for one: setup_inputs(seed, part) draws one part's arguments, and reference() takes and returns one part's arrays. A program takes and returns all parts, laid end to end along the dimension named above; an argument that names none is the same for every part. Nothing has to cross between parts.
All inputs are finite; a program needn't handle non-finite values.
Results may differ from the reference program's by a relative error of at most 0.0022.
Values may be sent and summed in bfloat16 or wider, within the bound.
No kernel may reach another device: no remote copies, remote signals or barrier semaphores. Data moves between devices by JAX's collectives and lax.ppermute only.
A program may use at most 128 MiB of HBM per device.

```python
import math
import jax
import jax.numpy as jnp
from jax import lax

ATOMS = 256
CHANNELS = 64
ATOM_LEN = 128
ITERS = 2
TIME_ALL = 8192


def draw_signal(key, part):
    key_noise, key_scale = jax.random.split(jax.random.fold_in(key, 11))
    positions = jnp.arange(TIME_ALL, dtype=jnp.float32)
    envelope = 2.0 * jnp.sqrt(1.0 + 2.0 * positions / TIME_ALL)
    noise_draw = jnp.clip(jax.random.normal(key_noise, (CHANNELS, TIME_ALL), jnp.float32), -4.0, 4.0)
    channel_scale = jnp.exp(jax.random.uniform(key_scale, (CHANNELS, 1), jnp.float32, math.log(0.5), math.log(2.0)))
    return (noise_draw * channel_scale * envelope[None, :]).astype(jnp.float32)


def normal_values(key, shape, width, most, held_as=jnp.bfloat16):
    entries = jax.random.normal(key, shape, jnp.float32) * width
    return jnp.minimum(jnp.maximum(entries, -most), most).astype(held_as)


def setup_inputs(seed: int = 0, part: int = 0) -> dict:
    splits = jax.random.split(jax.random.key(seed), 4)
    part_keys = jax.random.split(jax.random.fold_in(splits[3], part), 4)
    signal = draw_signal(jax.random.fold_in(jax.random.fold_in(splits[3], part), 71), part)
    dictionary = normal_values(splits[1], (ATOMS, CHANNELS, ATOM_LEN), 1.0, 4.0)
    step = jnp.clip(jax.random.uniform(splits[2], (1,), jnp.float32, 0.04, 0.08), 0.04, 0.08)
    return {"signal": signal, "dictionary": dictionary, "step": step}


SPARSITY = 0.05
DICT_RATE = 0.5
EPSILON = 1e-06

def convolve(inputs, kernel):
    return lax.conv_general_dilated(inputs[None], kernel, (1,), 'VALID', dimension_numbers=('NCH', 'OIH', 'NCH'), precision=lax.Precision.HIGHEST)[0]

def to_bf16(values):
    return values.astype(jnp.bfloat16)

def widen(values):
    return lax.optimization_barrier(values).astype(jnp.float32)

def reference(signal, dictionary, step):
    scale = 1.0 / math.sqrt(CHANNELS * ATOM_LEN)
    dict_wide = dictionary.astype(jnp.float32)
    flipped = jnp.transpose(jnp.flip(dict_wide, 2), (1, 0, 2))
    step_size = step[0]

    def forward_model(codes_low):
        padded = jnp.pad(widen(codes_low), ((0, 0), (ATOM_LEN - 1, 0)))
        return convolve(padded, flipped) * scale

    def adjoint_model(resid_low):
        padded = jnp.pad(widen(resid_low), ((0, 0), (0, ATOM_LEN - 1)))
        return convolve(padded, dict_wide) * scale
    current = jnp.zeros((ATOMS, TIME_ALL), jnp.float32)
    extrapolated = current
    momentum = 1.0
    threshold = jnp.float32(0.0)
    for iteration in range(ITERS):
        if iteration == 0:
            residual = -signal
        else:
            residual = forward_model(to_bf16(extrapolated)) - signal
        gradient = adjoint_model(to_bf16(residual))
        if iteration == 0:
            threshold = SPARSITY * jnp.max(jnp.abs(gradient))
        moved = extrapolated - step_size * gradient
        updated = jnp.sign(moved) * jnp.maximum(jnp.abs(moved) - step_size * threshold, 0.0)
        following = (1.0 + math.sqrt(1.0 + 4.0 * momentum * momentum)) / 2.0
        extrapolated = updated + (momentum - 1.0) / following * (updated - current)
        current = updated
        momentum = following
    codes_low = to_bf16(current)
    final_residual = forward_model(codes_low) - signal
    resid_wide = widen(to_bf16(final_residual))
    codes_padded = jnp.pad(widen(codes_low), ((0, 0), (ATOM_LEN - 1, 0)))

    def one_lag(lag):
        segment = lax.dynamic_slice_in_dim(codes_padded, (ATOM_LEN - 1 - lag).astype(jnp.int32), TIME_ALL, 1)
        return jnp.dot(segment, resid_wide.T, precision=lax.Precision.HIGHEST)
    lags = jnp.arange(ATOM_LEN, dtype=jnp.int32)
    atom_gradient = jnp.transpose(lax.map(one_lag, lags), (1, 2, 0))
    normed = atom_gradient / jnp.sqrt(lax.optimization_barrier(jnp.mean(atom_gradient * atom_gradient, axis=(1, 2), keepdims=True)) + EPSILON)
    shifted = dict_wide - DICT_RATE * normed
    new_dictionary = shifted / jnp.sqrt(lax.optimization_barrier(jnp.mean(shifted * shifted, axis=(1, 2), keepdims=True)) + EPSILON)
    loss = (0.5 * jnp.sum(final_residual * final_residual) + threshold * jnp.sum(jnp.abs(current))) / (CHANNELS * TIME_ALL)
    return (current, new_dictionary, loss.reshape(1))
```

```python
import math

import jax
import jax.numpy as jnp
from jax import lax
from jax.experimental import pallas as pl
from jax.experimental.pallas import tpu as pltpu
from jax.sharding import PartitionSpec as P

ATOMS = 256
CHANNELS = 64
ATOM_LEN = 128
SPARSITY = 0.05
DICT_RATE = 0.5
EPSILON = 1e-06

SCALE = 1.0 / math.sqrt(CHANNELS * ATOM_LEN)
FINE = 16
COARSE = ATOM_LEN // FINE
WIDE = FINE * CHANNELS
HALO = 2 * ATOM_LEN
F32 = jnp.float32
BF16 = jnp.bfloat16
VMEM_LIMIT = 56 * 1024 * 1024


def vmem():
    return pl.BlockSpec(memory_space=pltpu.VMEM)


def smem():
    return pl.BlockSpec(memory_space=pltpu.SMEM)


def kernel_params():
    return pltpu.CompilerParams(vmem_limit_bytes=VMEM_LIMIT)


def shifted(value, axis, steps):
    count = lax.axis_size(axis)
    leading, last = (max(0, -steps), min(count, count - steps))
    return lax.ppermute(value, axis, [(source, source + steps) for source in range(leading, last)])


def swapped(value, bit):
    count = lax.axis_size("tm")
    return lax.ppermute(value, "tm", [(i, i ^ bit) for i in range(count)])


def fill_windows(pairs, windows, rows):
    for step in range(FINE // 2):
        windows[0:rows, step * 128 : (step + 1) * 128] = pairs[
            2 * step : 2 * step + rows, :
        ].astype(BF16)


def adjoint(windows, lags, total, start, rows):
    for coarse in range(COARSE):
        part = jnp.dot(
            windows[start + coarse * FINE : start + coarse * FINE + rows, :],
            lags[coarse * WIDE : (coarse + 1) * WIDE, :],
            preferred_element_type=F32,
        )
        if coarse == 0:
            total[0:rows, :] = part
        else:
            total[0:rows, :] += part


def first_kernel(left, middle, right, lags, gradient, largest, pairs, windows):
    width = middle.shape[1]
    rows = width + 3 * ATOM_LEN
    whole = jnp.concatenate([left[...], middle[...], right[...]], 1)
    whole = -whole
    both = jnp.concatenate([whole, pltpu.roll(whole, whole.shape[1] - 1, 1)], 0)
    pairs[0 : width + 2 * HALO, :] = both.T
    fill_windows(pairs, windows, width + 2 * HALO - FINE)
    adjoint(windows, lags, gradient, 0, rows)
    own = jnp.abs(gradient[HALO : HALO + width, :]) * SCALE
    folded = jnp.max(own.reshape(width // 8, 8, ATOMS), 0)
    largest[...] = jnp.maximum(folded[:, :128], folded[:, 128:])


def forward(codes, lags, spread, start, rows, first):
    for coarse in range(COARSE):
        low = start - coarse * FINE
        part = lax.dot_general(
            codes[low : low + rows, :],
            lags[coarse * WIDE : (coarse + 1) * WIDE, :],
            (((1,), (1,)), ((), ())),
            preferred_element_type=F32,
        )
        if coarse == 0:
            spread[0:rows, :] = part
        else:
            spread[0:rows, :] += part
    keep = rows - FINE
    total = spread[FINE : FINE + keep, 0:128]
    odd = spread[FINE - 1 : FINE - 1 + keep, 0:128]
    for step in range(1, FINE // 2):
        lanes = slice(step * 128, (step + 1) * 128)
        total = total + spread[FINE - 2 * step : FINE - 2 * step + keep, lanes]
        odd = odd + spread[FINE - 1 - 2 * step : FINE - 1 - 2 * step + keep, lanes]
    return total[:, 0:64] + odd[:, 64:128]


def soft(moved, bound):
    return jnp.where(moved > 0, 1.0, -1.0) * jnp.maximum(jnp.abs(moved) - bound, 0.0)


def second_kernel(
    left, middle, right, lags, gradient, peak, step, valid,
    codes_out, ahead_out, resid_out, loss_out,
    signal, codes, codes_low, pairs, windows, spread,
):
    width = middle.shape[1]
    step_size = step[0]
    threshold = SPARSITY * jnp.max(peak[...])
    bound = step_size * threshold
    low, high = valid[0], valid[1]
    whole = jnp.concatenate([left[...], middle[...], right[...]], 1)
    signal[...] = whole.T

    def row(start, count):
        return lax.broadcasted_iota(jnp.int32, (count, 1), 0) + start

    rows1 = width + 3 * ATOM_LEN
    moved = -step_size * (gradient[...] * SCALE)
    updated = jnp.where(row(0, rows1) >= low, soft(moved, bound), 0.0)
    codes[...] = updated
    codes_low[...] = updated.astype(BF16)
    rows2 = width + 2 * ATOM_LEN
    model = forward(codes_low, lags, spread, ATOM_LEN - FINE, rows2 + FINE, 0)
    resid = model * SCALE - signal[ATOM_LEN : ATOM_LEN + rows2, :]
    resid = jnp.where(row(ATOM_LEN, rows2) < high, resid, 0.0)
    pairs[0:rows2, 0:64] = resid
    pairs[0 : rows2 - 1, 64:128] = pairs[1:rows2, 0:64]
    fill_windows(pairs, windows, rows2 - FINE)
    rows3 = width + ATOM_LEN
    adjoint(windows, lags, spread.at[:, 0:ATOMS], 0, rows3)
    before = codes[ATOM_LEN : ATOM_LEN + rows3, :]
    moved = before - step_size * (spread[0:rows3, 0:ATOMS] * SCALE)
    updated = jnp.where(row(ATOM_LEN, rows3) >= low, soft(moved, bound), 0.0)
    codes[0:rows3, :] = updated
    codes_low[0:rows3, :] = updated.astype(BF16)
    turned = updated.T
    ahead_out[...] = turned.astype(BF16)
    codes_out[...] = turned[:, ATOM_LEN:]
    sparse = jnp.sum(jnp.abs(codes[ATOM_LEN:rows3, :]))
    model = forward(codes_low, lags, spread, ATOM_LEN - FINE, width + FINE, 0)
    resid = model * SCALE - signal[HALO : HALO + width, :]
    resid_out[...] = resid.T.astype(BF16)
    loss = 0.5 * jnp.sum(resid * resid) + threshold * sparse
    loss_out[...] = jnp.full((8, 128), loss, F32)


def correlate_kernel(codes, resid, out, pairs, windows):
    blocks, atoms, length = codes.shape
    width = resid.shape[2]
    rows = width + 2 * FINE
    used = width + FINE
    pairs[...] = jnp.zeros_like(pairs)

    def one(block, carry):
        piece = resid[block].astype(F32)
        pairs[FINE : FINE + width, 0:64] = piece.T
        pairs[0 : FINE + width, 64:128] = pairs[1 : FINE + width + 1, 0:64]
        fill_windows(pairs, windows, used)
        held = codes[block].astype(F32)
        stack = []
        for coarse in range(COARSE):
            start = ATOM_LEN - FINE - coarse * FINE
            turned = held if start == 0 else pltpu.roll(held, length - start, 1)
            stack.append(turned[:, 0:used].astype(BF16))
        part = jnp.dot(jnp.concatenate(stack, 0), windows[0:used, :], preferred_element_type=F32)
        out[...] += part
        return carry

    out[...] = jnp.zeros_like(out)
    lax.fori_loop(0, blocks, one, 0)


def body(signal, dictionary, step):
    width = signal.shape[1]
    count = lax.axis_size("tm")
    me = lax.axis_index("tm")
    left = shifted(signal[:, width - HALO :], "tm", 1)
    right = shifted(signal[:, :HALO], "tm", -1)
    lags = jnp.transpose(dictionary, (2, 1, 0)).reshape(ATOM_LEN * CHANNELS, ATOMS)
    rows1 = width + 3 * ATOM_LEN
    span = width + 2 * HALO

    gradient, peak = pl.pallas_call(
        first_kernel,
        out_shape=(
            jax.ShapeDtypeStruct((rows1, ATOMS), F32),
            jax.ShapeDtypeStruct((8, 128), F32),
        ),
        in_specs=[vmem()] * 4,
        out_specs=(vmem(), vmem()),
        scratch_shapes=[pltpu.VMEM((span, 128), F32), pltpu.VMEM((span, WIDE), BF16)],
        compiler_params=kernel_params(),
    )(left, signal, right, lags)

    bit = 1
    while bit < count:
        peak = jnp.maximum(peak, swapped(peak, bit))
        bit *= 2

    valid = jnp.stack(
        [jnp.where(me == 0, HALO, 0), jnp.where(me == count - 1, HALO + width, span)]
    ).astype(jnp.int32)
    codes, ahead, resid, loss = pl.pallas_call(
        second_kernel,
        out_shape=(
            jax.ShapeDtypeStruct((ATOMS, width), F32),
            jax.ShapeDtypeStruct((ATOMS, width + ATOM_LEN), BF16),
            jax.ShapeDtypeStruct((CHANNELS, width), BF16),
            jax.ShapeDtypeStruct((8, 128), F32),
        ),
        in_specs=[vmem()] * 6 + [smem()] * 2,
        out_specs=(vmem(),) * 4,
        scratch_shapes=[
            pltpu.VMEM((span, CHANNELS), F32),
            pltpu.VMEM((rows1, ATOMS), F32),
            pltpu.VMEM((rows1, ATOMS), BF16),
            pltpu.VMEM((rows1, 128), F32),
            pltpu.VMEM((rows1, WIDE), BF16),
            pltpu.VMEM((rows1, WIDE), F32),
        ],
        compiler_params=kernel_params(),
    )(left, signal, right, lags, gradient, peak, step, valid)

    owned = ATOMS // count

    def correlate(codes_blocks, resid_blocks):
        atoms = codes_blocks.shape[1]
        out = pl.pallas_call(
            correlate_kernel,
            out_shape=jax.ShapeDtypeStruct((COARSE * atoms, WIDE), F32),
            in_specs=[vmem()] * 2,
            out_specs=vmem(),
            scratch_shapes=[
                pltpu.VMEM((width + 3 * FINE, 128), F32),
                pltpu.VMEM((width + 2 * FINE, WIDE), BF16),
            ],
            compiler_params=kernel_params(),
        )(codes_blocks, resid_blocks)
        return out.reshape(COARSE, atoms, WIDE)

    if count == 16:
        groups = [[2 * i + core for i in range(8)] for core in range(2)]
        pieces = jnp.concatenate(
            [
                ahead.reshape(8, 2 * owned, width + ATOM_LEN),
                jnp.broadcast_to(
                    jnp.pad(resid, ((0, 0), (0, ATOM_LEN)))[None],
                    (8, CHANNELS, width + ATOM_LEN),
                ),
            ],
            1,
        )
        taken = lax.all_to_all(pieces, "tm", 0, 0, axis_index_groups=groups, tiled=False)
        part = correlate(taken[:, : 2 * owned], taken[:, 2 * owned :, :width])
        core = me % 2
        give = lax.dynamic_slice_in_dim(part, (1 - core) * owned, owned, 1)
        keep = lax.dynamic_slice_in_dim(part, core * owned, owned, 1)
        summed = keep + swapped(give, 1)
    else:
        part = correlate(ahead[None], resid[None])
        summed = lax.psum_scatter(part, "tm", scatter_dimension=1, tiled=True)
    atom_gradient = (
        summed.reshape(COARSE, owned, FINE, CHANNELS)
        .transpose(1, 3, 0, 2)
        .reshape(owned, CHANNELS, ATOM_LEN)
    )
    own_atoms = lax.dynamic_slice_in_dim(dictionary, me * owned, owned, 0).astype(F32)
    normed = atom_gradient / jnp.sqrt(
        jnp.mean(atom_gradient * atom_gradient, axis=(1, 2), keepdims=True) + EPSILON
    )
    shifted_atoms = own_atoms - DICT_RATE * normed
    new_dictionary = shifted_atoms / jnp.sqrt(
        jnp.mean(shifted_atoms * shifted_atoms, axis=(1, 2), keepdims=True) + EPSILON
    )
    bit = 1
    while bit < count:
        loss = loss + swapped(loss, bit)
        bit *= 2
    loss = loss[0, :1] / (CHANNELS * width * count)
    return (codes, new_dictionary, loss)


def solution(mesh):
    return jax.shard_map(
        body,
        mesh=mesh,
        in_specs=(P(None, ("groups", "tm")), P(), P()),
        out_specs=(P(None, ("groups", "tm")), P(("groups", "tm"), None, None), P("groups")),
        check_vma=False,
    )
```

```python
import math

import jax
import jax.numpy as jnp
from jax import lax
from jax.experimental import pallas as pl
from jax.experimental.pallas import tpu as pltpu
from jax.sharding import PartitionSpec as P

ATOMS = 256
CHANNELS = 64
ATOM_LEN = 128
SPARSITY = 0.05
DICT_RATE = 0.5
EPSILON = 1e-06

SCALE = 1.0 / math.sqrt(CHANNELS * ATOM_LEN)
FINE = 16
COARSE = ATOM_LEN // FINE
WIDE = FINE * CHANNELS
HALO = 2 * ATOM_LEN
F32 = jnp.float32
BF16 = jnp.bfloat16
VMEM_LIMIT = 56 * 1024 * 1024


def vmem():
    return pl.BlockSpec(memory_space=pltpu.VMEM)


def smem():
    return pl.BlockSpec(memory_space=pltpu.SMEM)


def kernel_params():
    return pltpu.CompilerParams(vmem_limit_bytes=VMEM_LIMIT)


def shifted(value, axis, steps):
    count = lax.axis_size(axis)
    leading, last = (max(0, -steps), min(count, count - steps))
    return lax.ppermute(value, axis, [(source, source + steps) for source in range(leading, last)])


def swapped(value, bit):
    count = lax.axis_size("tm")
    return lax.ppermute(value, "tm", [(i, i ^ bit) for i in range(count)])


def fill_windows(pairs, windows, rows):
    for step in range(FINE // 2):
        windows[0:rows, step * 128 : (step + 1) * 128] = pairs[
            2 * step : 2 * step + rows, :
        ].astype(BF16)


def adjoint(windows, lags, total, start, rows):
    for coarse in range(COARSE):
        part = jnp.dot(
            windows[start + coarse * FINE : start + coarse * FINE + rows, :],
            lags[coarse * WIDE : (coarse + 1) * WIDE, :],
            preferred_element_type=F32,
        )
        if coarse == 0:
            total[0:rows, :] = part
        else:
            total[0:rows, :] += part


def first_kernel(left, middle, right, lags, gradient, largest, pairs, windows):
    width = middle.shape[1]
    rows = width + 3 * ATOM_LEN
    whole = jnp.concatenate([left[...], middle[...], right[...]], 1)
    whole = -whole
    both = jnp.concatenate([whole, pltpu.roll(whole, whole.shape[1] - 1, 1)], 0)
    pairs[0 : width + 2 * HALO, :] = both.T
    fill_windows(pairs, windows, width + 2 * HALO - FINE)
    adjoint(windows, lags, gradient, 0, rows)
    own = jnp.abs(gradient[HALO : HALO + width, :]) * SCALE
    folded = jnp.max(own.reshape(width // 8, 8, ATOMS), 0)
    largest[...] = jnp.maximum(folded[:, :128], folded[:, 128:])


def forward(codes, lags, wide, spread, folded, start, rows):
    for coarse in range(COARSE):
        low = start - coarse * FINE
        wide[0:rows, coarse * ATOMS : (coarse + 1) * ATOMS] = codes[low : low + rows, :]
    weights = jnp.concatenate(
        [lags[coarse * WIDE : (coarse + 1) * WIDE, :] for coarse in range(COARSE)], 1
    )
    spread[0:rows, :] = lax.dot_general(
        wide[0:rows, :], weights, (((1,), (1,)), ((), ())), preferred_element_type=F32
    )
    keep = rows - FINE
    total = spread[FINE - 2 : FINE - 2 + keep + 2, 0:128]
    for step in range(1, FINE // 2):
        lanes = slice(step * 128, (step + 1) * 128)
        low = FINE - 2 - 2 * step
        total = total + spread[low : low + keep + 2, lanes]
    folded[0 : keep + 2, :] = total
    return folded[2 : keep + 2, 0:64] + folded[1 : keep + 1, 64:128]


def soft(moved, bound):
    return jnp.where(moved > 0, 1.0, -1.0) * jnp.maximum(jnp.abs(moved) - bound, 0.0)


def second_kernel(
    left, middle, right, lags, gradient, peak, step, valid, *rest
):
    outs, (signal, codes, codes_low, pairs, windows, wide, spread, folded) = rest[:-8], rest[-8:]
    width = middle.shape[1]
    step_size = step[0]
    threshold = SPARSITY * jnp.max(peak[...])
    bound = step_size * threshold
    low, high = valid[0], valid[1]
    whole = jnp.concatenate([left[...], middle[...], right[...]], 1)
    signal[...] = whole.T

    def row(start, count):
        return lax.broadcasted_iota(jnp.int32, (count, 1), 0) + start

    rows1 = width + 3 * ATOM_LEN
    moved = -step_size * (gradient[...] * SCALE)
    updated = jnp.where(row(0, rows1) >= low, soft(moved, bound), 0.0)
    codes[...] = updated
    codes_low[...] = updated.astype(BF16)
    rows2 = width + 2 * ATOM_LEN
    model = forward(codes_low, lags, wide, spread, folded, ATOM_LEN - FINE, rows2 + FINE)
    resid = model * SCALE - signal[ATOM_LEN : ATOM_LEN + rows2, :]
    resid = jnp.where(row(ATOM_LEN, rows2) < high, resid, 0.0)
    pairs[0:rows2, 0:64] = resid
    pairs[0 : rows2 - 1, 64:128] = pairs[1:rows2, 0:64]
    fill_windows(pairs, windows, rows2 - FINE)
    rows3 = width + ATOM_LEN
    adjoint(windows, lags, spread.at[:, 0:ATOMS], 0, rows3)
    before = codes[ATOM_LEN : ATOM_LEN + rows3, :]
    moved = before - step_size * (spread[0:rows3, 0:ATOMS] * SCALE)
    updated = jnp.where(row(ATOM_LEN, rows3) >= low, soft(moved, bound), 0.0)
    codes[0:rows3, :] = updated
    codes_low[0:rows3, :] = updated.astype(BF16)
    turned = updated.T
    outs[0][...] = turned[:, ATOM_LEN:]
    sparse = jnp.sum(jnp.abs(codes[ATOM_LEN:rows3, :]))
    model = forward(codes_low, lags, wide, spread, folded, ATOM_LEN - FINE, width + FINE)
    resid = model * SCALE - signal[HALO : HALO + width, :]
    resid_low = resid.T.astype(BF16)
    ahead = turned.astype(BF16)
    loss = 0.5 * jnp.sum(resid * resid) + threshold * sparse
    if len(outs) == 2:
        peers, rows, _ = outs[1].shape
        atoms = rows - CHANNELS
        whole_loss = jnp.full((CHANNELS, ATOM_LEN), loss, F32)
        high_part = whole_loss.astype(BF16)
        rest_loss = whole_loss - high_part.astype(F32)
        middle_part = rest_loss.astype(BF16)
        low_part = (rest_loss - middle_part.astype(F32)).astype(BF16)
        lane = lax.broadcasted_iota(jnp.int32, (CHANNELS, ATOM_LEN), 1)
        tail = jnp.where(
            lane == 0,
            high_part.astype(F32),
            jnp.where(lane == 1, middle_part.astype(F32), low_part.astype(F32)),
        ).astype(BF16)
        for peer in range(peers):
            outs[1][peer, 0:atoms, :] = ahead[peer * atoms : (peer + 1) * atoms, :]
            outs[1][peer, atoms:rows, 0:width] = resid_low
            outs[1][peer, atoms:rows, width:] = tail
    else:
        outs[1][...] = ahead
        outs[2][...] = resid_low
        outs[3][...] = jnp.full((8, 128), loss, F32)


def correlate(codes_of, resid_of, blocks, atoms, width, stack, pairs, windows):
    main = blocks * width
    length = width + ATOM_LEN
    lane = lax.broadcasted_iota(jnp.int32, (atoms, ATOM_LEN), 1)
    extra = [jnp.zeros((atoms, ATOM_LEN), F32) for _ in range(COARSE)]
    windows[main : main + ATOM_LEN, :] = jnp.zeros((ATOM_LEN, WIDE), BF16)
    for block in range(blocks):
        piece = jnp.concatenate(
            [resid_of(block).astype(F32), jnp.zeros((CHANNELS, ATOM_LEN), F32)], 1
        )
        piece = pltpu.roll(piece, FINE, 1)
        both = jnp.concatenate([piece, pltpu.roll(piece, length - 1, 1)], 0)
        slot = pairs.at[block % 2]
        slot[...] = both.T
        for step in range(FINE // 2):
            lanes = slice(step * 128, (step + 1) * 128)
            low = 2 * step
            windows[main + block * FINE : main + (block + 1) * FINE, lanes] = slot[
                low : low + FINE, :
            ].astype(BF16)
            low += FINE
            windows[block * width : (block + 1) * width, lanes] = slot[
                low : low + width, :
            ].astype(BF16)
        held = codes_of(block).astype(F32)
        for coarse in range(COARSE):
            start = ATOM_LEN - coarse * FINE
            turned = pltpu.roll(held, length - start, 1)
            stack[coarse * atoms : (coarse + 1) * atoms, block * width : (block + 1) * width] = (
                turned[:, :width].astype(BF16)
            )
            turned = pltpu.roll(held, (FINE * block - (start - FINE)) % length, 1)[:, :ATOM_LEN]
            inside = (lane >= FINE * block) & (lane < FINE * (block + 1))
            extra[coarse] = jnp.where(inside, turned, extra[coarse])
    for coarse in range(COARSE):
        stack[coarse * atoms : (coarse + 1) * atoms, main : main + ATOM_LEN] = extra[coarse].astype(
            BF16
        )
    return jnp.dot(stack[...], windows[...], preferred_element_type=F32)


def shared_kernel(core, taken, keep, give, stack, pairs, windows, total):
    blocks, rows, length = taken.shape
    atoms = rows - CHANNELS
    width = length - ATOM_LEN
    half = atoms // 2
    total[...] = correlate(
        lambda b: taken[b, 0:atoms, :],
        lambda b: taken[b, atoms:rows, 0:width],
        blocks, atoms, width, stack, pairs, windows,
    )
    mine = core[0] * half
    other = half - mine
    for coarse in range(COARSE):
        rows_of = slice(coarse * half, (coarse + 1) * half)
        keep[rows_of, :] = total[pl.ds(coarse * atoms + mine, half), :]
        give[rows_of, :] = total[pl.ds(coarse * atoms + other, half), :]
    loss = jnp.zeros((16, ATOM_LEN), F32)
    for block in range(blocks):
        loss += taken[block, atoms : atoms + 16, width:].astype(F32)
    lane = lax.broadcasted_iota(jnp.int32, (16, ATOM_LEN), 1)
    loss = jnp.sum(jnp.where(lane < 3, loss, 0.0), 1, keepdims=True)[0:8]
    ending = jnp.broadcast_to(loss, (8, WIDE))
    keep[COARSE * half :, :] = ending
    give[COARSE * half :, :] = ending


def lone_kernel(codes, resid, out, stack, pairs, windows):
    out[...] = correlate(
        lambda b: codes[...], lambda b: resid[...], 1, ATOMS, resid.shape[1], stack, pairs, windows
    )


def last_kernel(inverse, keep, recv, atoms_ref, out, loss_out, total, turned):
    half = atoms_ref.shape[0]
    loss_out[0] = (keep[COARSE * half, 0] + recv[COARSE * half, 0]) * inverse
    for step in range(FINE // 2):
        lanes = slice(step * 128, (step + 1) * 128)
        total[step] = keep[0 : COARSE * half, lanes] + recv[0 : COARSE * half, lanes]
    for pair in range(half // 2):
        for step in range(FINE // 2):
            one = total.at[step][pl.ds(2 * pair, COARSE, stride=half), :]
            two = total.at[step][pl.ds(2 * pair + 1, COARSE, stride=half), :]
            block = turned.at[pair]
            block[pl.ds(2 * step, COARSE, stride=FINE), :] = jnp.concatenate(
                [one[:, 0:64], two[:, 0:64]], 1
            )
            block[pl.ds(2 * step + 1, COARSE, stride=FINE), :] = jnp.concatenate(
                [one[:, 64:128], two[:, 64:128]], 1
            )
    gradient = jnp.concatenate([turned[pair].T for pair in range(half // 2)], 0)
    gradient = gradient.reshape(half, CHANNELS, ATOM_LEN)
    normed = gradient / jnp.sqrt(
        jnp.mean(gradient * gradient, axis=(1, 2), keepdims=True) + EPSILON
    )
    moved = atoms_ref[...].astype(F32) - DICT_RATE * normed
    out[...] = moved / jnp.sqrt(jnp.mean(moved * moved, axis=(1, 2), keepdims=True) + EPSILON)


def body(signal, dictionary, step):
    width = signal.shape[1]
    count = lax.axis_size("tm")
    me = lax.axis_index("tm")
    left = shifted(signal[:, width - HALO :], "tm", 1)
    right = shifted(signal[:, :HALO], "tm", -1)
    lags = jnp.transpose(dictionary, (2, 1, 0)).reshape(ATOM_LEN * CHANNELS, ATOMS)
    rows1 = width + 3 * ATOM_LEN
    span = width + 2 * HALO

    gradient, peak = pl.pallas_call(
        first_kernel,
        out_shape=(
            jax.ShapeDtypeStruct((rows1, ATOMS), F32),
            jax.ShapeDtypeStruct((8, 128), F32),
        ),
        in_specs=[vmem()] * 4,
        out_specs=(vmem(), vmem()),
        scratch_shapes=[pltpu.VMEM((span, 128), F32), pltpu.VMEM((span, WIDE), BF16)],
        compiler_params=kernel_params(),
    )(left, signal, right, lags)

    bit = 1
    while bit < count:
        peak = jnp.maximum(peak, swapped(peak, bit))
        bit *= 2

    valid = jnp.stack(
        [jnp.where(me == 0, HALO, 0), jnp.where(me == count - 1, HALO + width, span)]
    ).astype(jnp.int32)
    owned = ATOMS // count
    peers = count // 2
    shared = owned == 16
    own_atoms = lax.dynamic_slice_in_dim(dictionary, me * owned, owned, 0)
    if shared:
        outs = (jax.ShapeDtypeStruct((peers, 2 * owned + CHANNELS, width + ATOM_LEN), BF16),)
    else:
        outs = (
            jax.ShapeDtypeStruct((ATOMS, width + ATOM_LEN), BF16),
            jax.ShapeDtypeStruct((CHANNELS, width), BF16),
            jax.ShapeDtypeStruct((8, 128), F32),
        )
    codes, *others = pl.pallas_call(
        second_kernel,
        out_shape=(jax.ShapeDtypeStruct((ATOMS, width), F32),) + outs,
        in_specs=[vmem()] * 6 + [smem()] * 2,
        out_specs=(vmem(),) * (1 + len(outs)),
        scratch_shapes=[
            pltpu.VMEM((span, CHANNELS), F32),
            pltpu.VMEM((rows1, ATOMS), F32),
            pltpu.VMEM((rows1, ATOMS), BF16),
            pltpu.VMEM((rows1, 128), F32),
            pltpu.VMEM((rows1, WIDE), BF16),
            pltpu.VMEM((rows1, COARSE * ATOMS), BF16),
            pltpu.VMEM((rows1, WIDE), F32),
            pltpu.VMEM((rows1, 128), F32),
        ],
        compiler_params=kernel_params(),
    )(left, signal, right, lags, gradient, peak, step, valid)

    def correlate_scratch(blocks, atoms):
        return [
            pltpu.VMEM((COARSE * atoms, blocks * width + ATOM_LEN), BF16),
            pltpu.VMEM((2, width + ATOM_LEN, 128), F32),
            pltpu.VMEM((blocks * width + ATOM_LEN, WIDE), BF16),
        ]

    inverse = 1.0 / (CHANNELS * width * count)
    if shared:
        core = me % 2
        groups = [[2 * i + c for i in range(peers)] for c in range(2)]
        taken = lax.all_to_all(others[0], "tm", 0, 0, axis_index_groups=groups, tiled=False)
        half_rows = jax.ShapeDtypeStruct((COARSE * owned + 8, WIDE), F32)
        keep, give = pl.pallas_call(
            shared_kernel,
            out_shape=(half_rows, half_rows),
            in_specs=[smem(), vmem()],
            out_specs=(vmem(), vmem()),
            scratch_shapes=correlate_scratch(peers, 2 * owned)
            + [pltpu.VMEM((COARSE * 2 * owned, WIDE), F32)],
            compiler_params=kernel_params(),
        )(core.reshape(1).astype(jnp.int32), taken)
        recv = swapped(give, 1)
        new_dictionary, loss = pl.pallas_call(
            lambda *refs: last_kernel(inverse, *refs),
            out_shape=(
                jax.ShapeDtypeStruct((owned, CHANNELS, ATOM_LEN), F32),
                jax.ShapeDtypeStruct((1,), F32),
            ),
            in_specs=[vmem()] * 3,
            out_specs=(vmem(), smem()),
            scratch_shapes=[
                pltpu.VMEM((FINE // 2, COARSE * owned, 128), F32),
                pltpu.VMEM((owned // 2, ATOM_LEN, 2 * CHANNELS), F32),
            ],
            compiler_params=kernel_params(),
        )(keep, recv, own_atoms)
        return (codes, new_dictionary, loss)

    ahead, resid, loss = others
    part = pl.pallas_call(
        lone_kernel,
        out_shape=jax.ShapeDtypeStruct((COARSE * ATOMS, WIDE), F32),
        in_specs=[vmem()] * 2,
        out_specs=vmem(),
        scratch_shapes=correlate_scratch(1, ATOMS),
        compiler_params=kernel_params(),
    )(ahead, resid)
    summed = lax.psum_scatter(
        part.reshape(COARSE, ATOMS, WIDE), "tm", scatter_dimension=1, tiled=True
    )
    atom_gradient = (
        summed.reshape(COARSE, owned, FINE, CHANNELS)
        .transpose(1, 3, 0, 2)
        .reshape(owned, CHANNELS, ATOM_LEN)
    )
    normed = atom_gradient / jnp.sqrt(
        jnp.mean(atom_gradient * atom_gradient, axis=(1, 2), keepdims=True) + EPSILON
    )
    moved = own_atoms.astype(F32) - DICT_RATE * normed
    new_dictionary = moved / jnp.sqrt(
        jnp.mean(moved * moved, axis=(1, 2), keepdims=True) + EPSILON
    )
    bit = 1
    while bit < count:
        loss = loss + swapped(loss, bit)
        bit *= 2
    return (codes, new_dictionary, loss[0, :1] * inverse)


def solution(mesh):
    return jax.shard_map(
        body,
        mesh=mesh,
        in_specs=(P(None, ("groups", "tm")), P(), P()),
        out_specs=(P(None, ("groups", "tm")), P(("groups", "tm"), None, None), P("groups")),
        check_vma=False,
    )
```

```python
import math

import jax
import jax.numpy as jnp
from jax import lax
from jax.experimental import pallas as pl
from jax.experimental.pallas import tpu as pltpu
from jax.sharding import PartitionSpec as P

ATOMS = 256
CHANNELS = 64
ATOM_LEN = 128
SPARSITY = 0.05
DICT_RATE = 0.5
EPSILON = 1e-06

SCALE = 1.0 / math.sqrt(CHANNELS * ATOM_LEN)
FINE = 16
COARSE = ATOM_LEN // FINE
WIDE = FINE * CHANNELS
HALO = 2 * ATOM_LEN
F32 = jnp.float32
BF16 = jnp.bfloat16
VMEM_LIMIT = 36 * 1024 * 1024


def vmem():
    return pl.BlockSpec(memory_space=pltpu.VMEM)


def smem():
    return pl.BlockSpec(memory_space=pltpu.SMEM)


def anywhere():
    return pl.BlockSpec(memory_space=pl.ANY)


def fetch_lags(source, lags, arrived):
    copies = [
        pltpu.make_async_copy(
            source.at[pl.ds(coarse * WIDE, WIDE), :],
            lags.at[pl.ds(coarse * WIDE, WIDE), :],
            arrived.at[coarse],
        )
        for coarse in range(COARSE)
    ]
    for copy in copies:
        copy.start()
    return copies


def cost(flops, bytes_accessed):
    return pl.CostEstimate(flops=flops, bytes_accessed=bytes_accessed, transcendentals=0)


def kernel_params(limit=VMEM_LIMIT):
    return pltpu.CompilerParams(vmem_limit_bytes=limit)


def shifted(value, axis, steps):
    count = lax.axis_size(axis)
    leading, last = (max(0, -steps), min(count, count - steps))
    return lax.ppermute(value, axis, [(source, source + steps) for source in range(leading, last)])


def swapped(value, bit):
    count = lax.axis_size("tm")
    return lax.ppermute(value, "tm", [(i, i ^ bit) for i in range(count)])


def fill_windows(pairs, windows, rows):
    for step in range(FINE // 2):
        windows[0:rows, step * 128 : (step + 1) * 128] = pairs[
            2 * step : 2 * step + rows, :
        ].astype(BF16)


def adjoint(windows, lags, total, spans, copies=None):
    rows = sum(count for _, count in spans)
    for coarse in range(COARSE):
        if copies is not None:
            copies[coarse].wait()
        shift = coarse * FINE
        taken = [windows[start + shift : start + shift + count, :] for start, count in spans]
        part = jnp.dot(
            taken[0] if len(taken) == 1 else jnp.concatenate(taken, 0),
            lags[coarse * WIDE : (coarse + 1) * WIDE, :],
            preferred_element_type=F32,
        )
        if coarse == 0:
            total[0:rows, :] = part
        else:
            total[0:rows, :] += part


def windows_of(whole, pairs, windows):
    length = whole.shape[1]
    both = jnp.concatenate([whole, pltpu.roll(whole, length - 1, 1)], 0)
    pairs[0:length, :] = both.T
    fill_windows(pairs, windows, length - FINE)


def own_kernel(middle, right_any, lags, gradient, largest, right, pairs, windows, sems):
    width = middle.shape[1]
    near = pltpu.make_async_copy(right_any, right, sems.at[COARSE])
    near.start()
    near.wait()
    whole = jnp.concatenate([middle[...], right[:, 0:ATOM_LEN]], 1)
    windows_of(-whole, pairs, windows)
    adjoint(windows, lags, gradient, [(0, width)])
    own = jnp.abs(gradient[...]) * SCALE
    folded = jnp.max(own.reshape(width // 8, 8, ATOMS), 0)
    folded = jnp.maximum(folded[:, :128], folded[:, 128:])
    for peer in range(largest.shape[0]):
        largest[peer] = folded


def border_kernel(
    left_any, middle, right_any, lags, gradient, lags_out, left, right, pairs, windows, sems
):
    near = [
        pltpu.make_async_copy(left_any, left, sems.at[COARSE]),
        pltpu.make_async_copy(right_any, right, sems.at[COARSE + 1]),
    ]
    for copy in near:
        copy.start()
    copies = fetch_lags(lags, lags_out, sems)
    for copy in near:
        copy.wait()
    whole = jnp.concatenate([left[...], middle[:, 0:ATOM_LEN], right[...]], 1)
    windows_of(-whole, pairs, windows)
    adjoint(windows, lags, gradient, [(0, HALO), (HALO + ATOM_LEN, ATOM_LEN)])
    for copy in copies:
        copy.wait()


def forward(codes, lags, wide, spread, folded, start, rows):
    for coarse in range(COARSE):
        low = start - coarse * FINE
        wide[0:rows, coarse * ATOMS : (coarse + 1) * ATOMS] = codes[low : low + rows, :]
    weights = jnp.concatenate(
        [lags[coarse * WIDE : (coarse + 1) * WIDE, :] for coarse in range(COARSE)], 1
    )
    spread[0:rows, :] = lax.dot_general(
        wide[0:rows, :], weights, (((1,), (1,)), ((), ())), preferred_element_type=F32
    )
    keep = rows - FINE
    total = spread[FINE - 2 : FINE - 2 + keep + 2, 0:128]
    for step in range(1, FINE // 2):
        lanes = slice(step * 128, (step + 1) * 128)
        low = FINE - 2 - 2 * step
        total = total + spread[low : low + keep + 2, lanes]
    folded[0 : keep + 2, :] = total
    return folded[2 : keep + 2, 0:64] + folded[1 : keep + 1, 64:128]


def soft(moved, bound):
    return jnp.where(moved > 0, 1.0, -1.0) * jnp.maximum(jnp.abs(moved) - bound, 0.0)


def second_kernel(
    left_any, middle, right_any, lags, own_gradient, border, peak, step, valid, *rest
):
    outs, scratch = rest[:-11], rest[-11:]
    signal, codes, codes_low, pairs, windows, wide, spread, folded = scratch[:8]
    left, right, sems = scratch[8:]
    near = [
        pltpu.make_async_copy(left_any, left, sems.at[COARSE]),
        pltpu.make_async_copy(right_any, right, sems.at[COARSE + 1]),
    ]
    for copy in near:
        copy.start()
    for copy in near:
        copy.wait()
    width = middle.shape[1]
    step_size = step[0]
    threshold = SPARSITY * jnp.max(peak[...])
    bound = step_size * threshold
    low, high = valid[0], valid[1]
    whole = jnp.concatenate([left[...], middle[...], right[...]], 1)
    signal[...] = whole.T

    def row(start, count):
        return lax.broadcasted_iota(jnp.int32, (count, 1), 0) + start

    for start, values in (
        (0, border[0:HALO, :]),
        (HALO, own_gradient[...]),
        (HALO + width, border[HALO:, :]),
    ):
        count = values.shape[0]
        moved = -step_size * (values * SCALE)
        updated = soft(moved, bound)
        if start == 0:
            updated = jnp.where(row(0, count) >= low, updated, 0.0)
        codes[start : start + count, :] = updated
        codes_low[start : start + count, :] = updated.astype(BF16)
    rows2 = width + 2 * ATOM_LEN
    model = forward(codes_low, lags, wide, spread, folded, ATOM_LEN - FINE, rows2 + FINE)
    resid = model * SCALE - signal[ATOM_LEN : ATOM_LEN + rows2, :]
    resid = jnp.where(row(ATOM_LEN, rows2) < high, resid, 0.0)
    pairs[0:rows2, 0:64] = resid
    pairs[0 : rows2 - 1, 64:128] = pairs[1:rows2, 0:64]
    fill_windows(pairs, windows, rows2 - FINE)
    rows3 = width + ATOM_LEN
    adjoint(windows, lags, spread.at[:, 0:ATOMS], [(0, rows3)])
    before = codes[ATOM_LEN : ATOM_LEN + rows3, :]
    moved = before - step_size * (spread[0:rows3, 0:ATOMS] * SCALE)
    updated = jnp.where(row(ATOM_LEN, rows3) >= low, soft(moved, bound), 0.0)
    codes[0:rows3, :] = updated
    codes_low[0:rows3, :] = updated.astype(BF16)
    turned = updated.T
    outs[0][...] = turned[:, ATOM_LEN:]
    sparse = jnp.sum(jnp.abs(codes[ATOM_LEN:rows3, :]))
    model = forward(codes_low, lags, wide, spread, folded, ATOM_LEN - FINE, width + FINE)
    resid = model * SCALE - signal[HALO : HALO + width, :]
    resid_low = resid.T.astype(BF16)
    ahead = turned.astype(BF16)
    loss = 0.5 * jnp.sum(resid * resid) + threshold * sparse
    if len(outs) == 2:
        peers, rows, _ = outs[1].shape
        atoms = rows - CHANNELS
        whole_loss = jnp.full((CHANNELS, ATOM_LEN), loss, F32)
        high_part = whole_loss.astype(BF16)
        rest_loss = whole_loss - high_part.astype(F32)
        middle_part = rest_loss.astype(BF16)
        low_part = (rest_loss - middle_part.astype(F32)).astype(BF16)
        lane = lax.broadcasted_iota(jnp.int32, (CHANNELS, ATOM_LEN), 1)
        tail = jnp.where(
            lane == 0,
            high_part.astype(F32),
            jnp.where(lane == 1, middle_part.astype(F32), low_part.astype(F32)),
        ).astype(BF16)
        for peer in range(peers):
            outs[1][peer, 0:atoms, :] = ahead[peer * atoms : (peer + 1) * atoms, :]
            outs[1][peer, atoms:rows, 0:width] = resid_low
            outs[1][peer, atoms:rows, width:] = tail
    else:
        outs[1][...] = ahead
        outs[2][...] = resid_low
        outs[3][...] = jnp.full((8, 128), loss, F32)


def correlate(codes_of, resid_of, blocks, atoms, width, stack, pairs, windows):
    main = blocks * width
    length = width + ATOM_LEN
    lane = lax.broadcasted_iota(jnp.int32, (atoms, ATOM_LEN), 1)
    extra = [jnp.zeros((atoms, ATOM_LEN), F32) for _ in range(COARSE)]
    windows[main : main + ATOM_LEN, :] = jnp.zeros((ATOM_LEN, WIDE), BF16)
    for block in range(blocks):
        piece = jnp.concatenate(
            [resid_of(block).astype(F32), jnp.zeros((CHANNELS, ATOM_LEN), F32)], 1
        )
        piece = pltpu.roll(piece, FINE, 1)
        both = jnp.concatenate([piece, pltpu.roll(piece, length - 1, 1)], 0)
        slot = pairs.at[block % 2]
        slot[...] = both.T
        for step in range(FINE // 2):
            lanes = slice(step * 128, (step + 1) * 128)
            low = 2 * step
            windows[main + block * FINE : main + (block + 1) * FINE, lanes] = slot[
                low : low + FINE, :
            ].astype(BF16)
            low += FINE
            windows[block * width : (block + 1) * width, lanes] = slot[
                low : low + width, :
            ].astype(BF16)
        held = codes_of(block).astype(F32)
        for coarse in range(COARSE):
            start = ATOM_LEN - coarse * FINE
            turned = pltpu.roll(held, length - start, 1)
            stack[coarse * atoms : (coarse + 1) * atoms, block * width : (block + 1) * width] = (
                turned[:, :width].astype(BF16)
            )
            turned = pltpu.roll(held, (FINE * block - (start - FINE)) % length, 1)[:, :ATOM_LEN]
            inside = (lane >= FINE * block) & (lane < FINE * (block + 1))
            extra[coarse] = jnp.where(inside, turned, extra[coarse])
    for coarse in range(COARSE):
        stack[coarse * atoms : (coarse + 1) * atoms, main : main + ATOM_LEN] = extra[coarse].astype(
            BF16
        )
    return jnp.dot(stack[...], windows[...], preferred_element_type=F32)


def shared_kernel(core, taken_any, keep, give, stack, pairs, windows, total, taken, sems):
    blocks, rows, length = taken.shape
    copies = [
        pltpu.make_async_copy(taken_any.at[block], taken.at[block], sems.at[block])
        for block in range(blocks)
    ]
    for copy in copies:
        copy.start()
    for copy in copies:
        copy.wait()
    atoms = rows - CHANNELS
    width = length - ATOM_LEN
    half = atoms // 2
    total[...] = correlate(
        lambda b: taken[b, 0:atoms, :],
        lambda b: taken[b, atoms:rows, 0:width],
        blocks, atoms, width, stack, pairs, windows,
    )
    mine = core[0] * half
    other = half - mine
    for coarse in range(COARSE):
        rows_of = slice(coarse * half, (coarse + 1) * half)
        keep[rows_of, :] = total[pl.ds(coarse * atoms + mine, half), :]
        give[rows_of, :] = total[pl.ds(coarse * atoms + other, half), :]
    loss = jnp.zeros((16, ATOM_LEN), F32)
    for block in range(blocks):
        loss += taken[block, atoms : atoms + 16, width:].astype(F32)
    lane = lax.broadcasted_iota(jnp.int32, (16, ATOM_LEN), 1)
    loss = jnp.sum(jnp.where(lane < 3, loss, 0.0), 1, keepdims=True)[0:8]
    ending = jnp.broadcast_to(loss, (8, WIDE))
    keep[COARSE * half :, :] = ending
    give[COARSE * half :, :] = ending


def lone_kernel(codes, resid, out, stack, pairs, windows):
    out[...] = correlate(
        lambda b: codes[...], lambda b: resid[...], 1, ATOMS, resid.shape[1], stack, pairs, windows
    )


def last_kernel(inverse, keep, recv_any, atoms_ref, out, loss_out, total, turned, recv, sem):
    copy = pltpu.make_async_copy(recv_any, recv, sem.at[0])
    copy.start()
    copy.wait()
    half = atoms_ref.shape[0]
    loss_out[0] = (keep[COARSE * half, 0] + recv[COARSE * half, 0]) * inverse
    for step in range(FINE // 2):
        lanes = slice(step * 128, (step + 1) * 128)
        total[step] = keep[0 : COARSE * half, lanes] + recv[0 : COARSE * half, lanes]
    for pair in range(half // 2):
        for step in range(FINE // 2):
            one = total.at[step][pl.ds(2 * pair, COARSE, stride=half), :]
            two = total.at[step][pl.ds(2 * pair + 1, COARSE, stride=half), :]
            block = turned.at[pair]
            block[pl.ds(2 * step, COARSE, stride=FINE), :] = jnp.concatenate(
                [one[:, 0:64], two[:, 0:64]], 1
            )
            block[pl.ds(2 * step + 1, COARSE, stride=FINE), :] = jnp.concatenate(
                [one[:, 64:128], two[:, 64:128]], 1
            )
    gradient = jnp.concatenate([turned[pair].T for pair in range(half // 2)], 0)
    gradient = gradient.reshape(half, CHANNELS, ATOM_LEN)
    normed = gradient / jnp.sqrt(
        jnp.mean(gradient * gradient, axis=(1, 2), keepdims=True) + EPSILON
    )
    moved = atoms_ref[...].astype(F32) - DICT_RATE * normed
    out[...] = moved / jnp.sqrt(jnp.mean(moved * moved, axis=(1, 2), keepdims=True) + EPSILON)


def body(signal, dictionary, step):
    width = signal.shape[1]
    count = lax.axis_size("tm")
    me = lax.axis_index("tm")
    left = shifted(signal[:, width - HALO :], "tm", 1)
    right = shifted(signal[:, :HALO], "tm", -1)
    lags = jnp.transpose(dictionary, (2, 1, 0)).reshape(ATOM_LEN * CHANNELS, ATOMS)
    rows1 = width + 3 * ATOM_LEN
    span = width + 2 * HALO

    near_scratch = [pltpu.VMEM((CHANNELS, HALO), F32)]
    sems = [pltpu.SemaphoreType.DMA((COARSE + 2,))]
    bordered = width + ATOM_LEN
    gradient, peak = pl.pallas_call(
        own_kernel,
        out_shape=(
            jax.ShapeDtypeStruct((width, ATOMS), F32),
            jax.ShapeDtypeStruct((count, 8, 128), F32),
        ),
        in_specs=[vmem(), anywhere(), vmem()],
        out_specs=(vmem(),) * 2,
        scratch_shapes=near_scratch
        + [pltpu.VMEM((bordered, 128), F32), pltpu.VMEM((bordered, WIDE), BF16)]
        + sems,
        compiler_params=kernel_params(),
        cost_estimate=cost(2 * width * ATOMS * WIDE * COARSE, 5 << 20),
    )(signal, right, lags)
    peak = lax.all_to_all(peak, "tm", 0, 0, tiled=False)
    span_border = 2 * HALO + ATOM_LEN
    border, lags = pl.pallas_call(
        border_kernel,
        out_shape=(
            jax.ShapeDtypeStruct((HALO + ATOM_LEN, ATOMS), F32),
            jax.ShapeDtypeStruct(lags.shape, BF16),
        ),
        in_specs=[anywhere(), vmem(), anywhere(), vmem()],
        out_specs=(vmem(), vmem()),
        scratch_shapes=near_scratch * 2
        + [pltpu.VMEM((span_border, 128), F32), pltpu.VMEM((span_border, WIDE), BF16)]
        + sems,
        compiler_params=kernel_params(),
        cost_estimate=cost(2 * (HALO + ATOM_LEN) * ATOMS * WIDE * COARSE, 5 << 20),
    )(left, signal, right, lags)

    valid = jnp.stack(
        [jnp.where(me == 0, HALO, 0), jnp.where(me == count - 1, HALO + width, span)]
    ).astype(jnp.int32)
    owned = ATOMS // count
    peers = count // 2
    shared = owned == 16
    own_atoms = lax.dynamic_slice_in_dim(dictionary, me * owned, owned, 0)
    if shared:
        outs = (jax.ShapeDtypeStruct((peers, 2 * owned + CHANNELS, width + ATOM_LEN), BF16),)
    else:
        outs = (
            jax.ShapeDtypeStruct((ATOMS, width + ATOM_LEN), BF16),
            jax.ShapeDtypeStruct((CHANNELS, width), BF16),
            jax.ShapeDtypeStruct((8, 128), F32),
        )
    codes, *others = pl.pallas_call(
        second_kernel,
        out_shape=(jax.ShapeDtypeStruct((ATOMS, width), F32),) + outs,
        in_specs=[anywhere(), vmem(), anywhere(), vmem()] + [vmem()] * 3 + [smem()] * 2,
        out_specs=(vmem(),) * (1 + len(outs)),
        scratch_shapes=[
            pltpu.VMEM((span, CHANNELS), F32),
            pltpu.VMEM((rows1, ATOMS), F32),
            pltpu.VMEM((rows1, ATOMS), BF16),
            pltpu.VMEM((rows1, 128), F32),
            pltpu.VMEM((rows1, WIDE), BF16),
            pltpu.VMEM((rows1, COARSE * ATOMS), BF16),
            pltpu.VMEM((rows1, WIDE), F32),
            pltpu.VMEM((rows1, 128), F32),
        ]
        + near_scratch * 2
        + sems,
        compiler_params=kernel_params(),
    )(left, signal, right, lags, gradient, border, peak, step, valid)

    def correlate_scratch(blocks, atoms):
        return [
            pltpu.VMEM((COARSE * atoms, blocks * width + ATOM_LEN), BF16),
            pltpu.VMEM((2, width + ATOM_LEN, 128), F32),
            pltpu.VMEM((blocks * width + ATOM_LEN, WIDE), BF16),
        ]

    inverse = 1.0 / (CHANNELS * width * count)
    if shared:
        core = me % 2
        groups = [[2 * i + c for i in range(peers)] for c in range(2)]
        taken = lax.all_to_all(others[0], "tm", 0, 0, axis_index_groups=groups, tiled=False)
        half_rows = jax.ShapeDtypeStruct((COARSE * owned + 8, WIDE), F32)
        keep, give = pl.pallas_call(
            shared_kernel,
            out_shape=(half_rows, half_rows),
            in_specs=[smem(), anywhere()],
            out_specs=(vmem(), vmem()),
            scratch_shapes=correlate_scratch(peers, 2 * owned)
            + [
                pltpu.VMEM((COARSE * 2 * owned, WIDE), F32),
                pltpu.VMEM(taken.shape, BF16),
                pltpu.SemaphoreType.DMA((peers,)),
            ],
            compiler_params=kernel_params(),
        )(core.reshape(1).astype(jnp.int32), taken)
        recv = swapped(give, 1)
        new_dictionary, loss = pl.pallas_call(
            lambda *refs: last_kernel(inverse, *refs),
            out_shape=(
                jax.ShapeDtypeStruct((owned, CHANNELS, ATOM_LEN), F32),
                jax.ShapeDtypeStruct((1,), F32),
            ),
            in_specs=[vmem(), anywhere(), vmem()],
            out_specs=(vmem(), smem()),
            scratch_shapes=[
                pltpu.VMEM((FINE // 2, COARSE * owned, 128), F32),
                pltpu.VMEM((owned // 2, ATOM_LEN, 2 * CHANNELS), F32),
                pltpu.VMEM(half_rows.shape, F32),
                pltpu.SemaphoreType.DMA((1,)),
            ],
            compiler_params=kernel_params(),
        )(keep, recv, own_atoms)
        return (codes, new_dictionary, loss)

    ahead, resid, loss = others
    part = pl.pallas_call(
        lone_kernel,
        out_shape=jax.ShapeDtypeStruct((COARSE * ATOMS, WIDE), F32),
        in_specs=[vmem()] * 2,
        out_specs=vmem(),
        scratch_shapes=correlate_scratch(1, ATOMS),
        compiler_params=kernel_params(),
    )(ahead, resid)
    summed = lax.psum_scatter(
        part.reshape(COARSE, ATOMS, WIDE), "tm", scatter_dimension=1, tiled=True
    )
    atom_gradient = (
        summed.reshape(COARSE, owned, FINE, CHANNELS)
        .transpose(1, 3, 0, 2)
        .reshape(owned, CHANNELS, ATOM_LEN)
    )
    normed = atom_gradient / jnp.sqrt(
        jnp.mean(atom_gradient * atom_gradient, axis=(1, 2), keepdims=True) + EPSILON
    )
    moved = own_atoms.astype(F32) - DICT_RATE * normed
    new_dictionary = moved / jnp.sqrt(
        jnp.mean(moved * moved, axis=(1, 2), keepdims=True) + EPSILON
    )
    bit = 1
    while bit < count:
        loss = loss + swapped(loss, bit)
        bit *= 2
    return (codes, new_dictionary, loss[0, :1] * inverse)


def solution(mesh):
    return jax.shard_map(
        body,
        mesh=mesh,
        in_specs=(P(None, ("groups", "tm")), P(), P()),
        out_specs=(P(None, ("groups", "tm")), P(("groups", "tm"), None, None), P("groups")),
        check_vma=False,
    )
```

```python
import math

import jax
import jax.numpy as jnp
from jax import lax
from jax.experimental import pallas as pl
from jax.experimental.pallas import tpu as pltpu
from jax.sharding import PartitionSpec as P

ATOMS = 256
CHANNELS = 64
ATOM_LEN = 128
SPARSITY = 0.05
DICT_RATE = 0.5
EPSILON = 1e-06

SCALE = 1.0 / math.sqrt(CHANNELS * ATOM_LEN)
FINE = 16
COARSE = ATOM_LEN // FINE
WIDE = FINE * CHANNELS
HALO = 2 * ATOM_LEN
F32 = jnp.float32
BF16 = jnp.bfloat16
PEERS = 8
VMEM_LIMIT = 36 * 1024 * 1024


def vmem():
    return pl.BlockSpec(memory_space=pltpu.VMEM)


def smem():
    return pl.BlockSpec(memory_space=pltpu.SMEM)


def anywhere():
    return pl.BlockSpec(memory_space=pl.ANY)


def fetch_lags(source, lags, arrived):
    copies = [
        pltpu.make_async_copy(
            source.at[pl.ds(coarse * WIDE, WIDE), :],
            lags.at[pl.ds(coarse * WIDE, WIDE), :],
            arrived.at[coarse],
        )
        for coarse in range(COARSE)
    ]
    for copy in copies:
        copy.start()
    return copies


def cost(flops, bytes_accessed):
    return pl.CostEstimate(flops=flops, bytes_accessed=bytes_accessed, transcendentals=0)


def kernel_params(limit=VMEM_LIMIT):
    return pltpu.CompilerParams(vmem_limit_bytes=limit)


def shifted(value, axis, steps):
    count = lax.axis_size(axis)
    leading, last = (max(0, -steps), min(count, count - steps))
    return lax.ppermute(value, axis, [(source, source + steps) for source in range(leading, last)])


def swapped(value, bit):
    count = lax.axis_size("tm")
    return lax.ppermute(value, "tm", [(i, i ^ bit) for i in range(count)])


def fill_windows(pairs, windows, rows):
    for step in range(FINE // 2):
        windows[0:rows, step * 128 : (step + 1) * 128] = pairs[
            2 * step : 2 * step + rows, :
        ].astype(BF16)


def adjoint(windows, lags, total, spans, copies=None):
    rows = sum(count for _, count in spans)
    for coarse in range(COARSE):
        if copies is not None:
            copies[coarse].wait()
        shift = coarse * FINE
        taken = [windows[start + shift : start + shift + count, :] for start, count in spans]
        part = jnp.dot(
            taken[0] if len(taken) == 1 else jnp.concatenate(taken, 0),
            lags[coarse * WIDE : (coarse + 1) * WIDE, :],
            preferred_element_type=F32,
        )
        if coarse == 0:
            total[0:rows, :] = part
        else:
            total[0:rows, :] += part


def windows_of(whole, pairs, windows):
    length = whole.shape[1]
    both = jnp.concatenate([whole, pltpu.roll(whole, length - 1, 1)], 0)
    pairs[0:length, :] = both.T
    fill_windows(pairs, windows, length - FINE)


def own_kernel(middle, right_any, lags, gradient, largest, right, pairs, windows, sems):
    width = middle.shape[1]
    near = pltpu.make_async_copy(right_any, right, sems.at[COARSE])
    near.start()
    near.wait()
    whole = jnp.concatenate([middle[...], right[:, 0:ATOM_LEN]], 1)
    windows_of(-whole, pairs, windows)
    adjoint(windows, lags, gradient, [(0, width)])
    own = jnp.abs(gradient[...]) * SCALE
    folded = jnp.max(own.reshape(width // 8, 8, ATOMS), 0)
    folded = jnp.maximum(folded[:, :128], folded[:, 128:])
    for peer in range(largest.shape[0]):
        largest[peer] = folded


def border_kernel(
    left_any, middle, right_any, lags, gradient, lags_out, left, right, pairs, windows, sems
):
    near = [
        pltpu.make_async_copy(left_any, left, sems.at[COARSE]),
        pltpu.make_async_copy(right_any, right, sems.at[COARSE + 1]),
    ]
    for copy in near:
        copy.start()
    copies = fetch_lags(lags, lags_out, sems)
    for copy in near:
        copy.wait()
    whole = jnp.concatenate([left[...], middle[:, 0:ATOM_LEN], right[...]], 1)
    windows_of(-whole, pairs, windows)
    adjoint(windows, lags, gradient, [(0, HALO), (HALO + ATOM_LEN, ATOM_LEN)])
    for copy in copies:
        copy.wait()


def forward(codes, lags, wide, spread, folded, start, rows):
    for coarse in range(COARSE):
        low = start - coarse * FINE
        wide[0:rows, coarse * ATOMS : (coarse + 1) * ATOMS] = codes[low : low + rows, :]
    weights = jnp.concatenate(
        [lags[coarse * WIDE : (coarse + 1) * WIDE, :] for coarse in range(COARSE)], 1
    )
    spread[0:rows, :] = lax.dot_general(
        wide[0:rows, :], weights, (((1,), (1,)), ((), ())), preferred_element_type=F32
    )
    keep = rows - FINE
    total = spread[FINE - 2 : FINE - 2 + keep + 2, 0:128]
    for step in range(1, FINE // 2):
        lanes = slice(step * 128, (step + 1) * 128)
        low = FINE - 2 - 2 * step
        total = total + spread[low : low + keep + 2, lanes]
    folded[0 : keep + 2, :] = total
    return folded[2 : keep + 2, 0:64] + folded[1 : keep + 1, 64:128]


def soft(moved, bound):
    return jnp.where(moved > 0, 1.0, -1.0) * jnp.maximum(jnp.abs(moved) - bound, 0.0)


def second_kernel(
    left_any, middle, right_any, lags, own_gradient, border, peak, step, valid, *rest
):
    outs, scratch, kept = rest[:-12], rest[-12:-1], rest[-1]
    signal, codes, codes_low, pairs, windows, wide, spread, folded = scratch[:8]
    left, right, sems = scratch[8:]
    near = [
        pltpu.make_async_copy(left_any, left, sems.at[COARSE]),
        pltpu.make_async_copy(right_any, right, sems.at[COARSE + 1]),
    ]
    for copy in near:
        copy.start()
    for copy in near:
        copy.wait()
    width = middle.shape[1]
    step_size = step[0]
    threshold = SPARSITY * jnp.max(peak[...])
    bound = step_size * threshold
    low, high = valid[0], valid[1]
    whole = jnp.concatenate([left[...], middle[...], right[...]], 1)
    signal[...] = whole.T

    def row(start, count):
        return lax.broadcasted_iota(jnp.int32, (count, 1), 0) + start

    for start, values in (
        (0, border[0:HALO, :]),
        (HALO, own_gradient[...]),
        (HALO + width, border[HALO:, :]),
    ):
        count = values.shape[0]
        moved = -step_size * (values * SCALE)
        updated = soft(moved, bound)
        if start == 0:
            updated = jnp.where(row(0, count) >= low, updated, 0.0)
        codes[start : start + count, :] = updated
        codes_low[start : start + count, :] = updated.astype(BF16)
    rows2 = width + 2 * ATOM_LEN
    model = forward(codes_low, lags, wide, spread, folded, ATOM_LEN - FINE, rows2 + FINE)
    resid = model * SCALE - signal[ATOM_LEN : ATOM_LEN + rows2, :]
    resid = jnp.where(row(ATOM_LEN, rows2) < high, resid, 0.0)
    pairs[0:rows2, 0:64] = resid
    pairs[0 : rows2 - 1, 64:128] = pairs[1:rows2, 0:64]
    fill_windows(pairs, windows, rows2 - FINE)
    rows3 = width + ATOM_LEN
    adjoint(windows, lags, spread.at[:, 0:ATOMS], [(0, rows3)])
    before = codes[ATOM_LEN : ATOM_LEN + rows3, :]
    moved = before - step_size * (spread[0:rows3, 0:ATOMS] * SCALE)
    updated = jnp.where(row(ATOM_LEN, rows3) >= low, soft(moved, bound), 0.0)
    codes[0:rows3, :] = updated
    codes_low[0:rows3, :] = updated.astype(BF16)
    turned = updated.T
    outs[0][...] = turned[:, ATOM_LEN:]
    sparse = jnp.sum(jnp.abs(codes[ATOM_LEN:rows3, :]))
    model = forward(codes_low, lags, wide, spread, folded, ATOM_LEN - FINE, width + FINE)
    resid = model * SCALE - signal[HALO : HALO + width, :]
    resid_low = resid.T.astype(BF16)
    ahead = turned.astype(BF16)
    loss = 0.5 * jnp.sum(resid * resid) + threshold * sparse
    if len(outs) == 1 + PEERS:
        atoms = ATOMS // PEERS
        whole_loss = jnp.full((16, ATOM_LEN), loss, F32)
        high_part = whole_loss.astype(BF16)
        rest_loss = whole_loss - high_part.astype(F32)
        middle_part = rest_loss.astype(BF16)
        low_part = (rest_loss - middle_part.astype(F32)).astype(BF16)
        lane = lax.broadcasted_iota(jnp.int32, (16, ATOM_LEN), 1)
        tail = jnp.where(
            lane == 0,
            high_part.astype(F32),
            jnp.where(lane == 1, middle_part.astype(F32), low_part.astype(F32)),
        ).astype(BF16)
        kept[...] = ahead
        for turn in range(PEERS):
            first = pl.multiple_of(valid[2 + turn] * atoms, atoms)
            piece = outs[1 + turn]
            piece[0:atoms, :] = kept[pl.ds(first, atoms), ATOM_LEN:]
            piece[atoms : atoms + CHANNELS, :] = resid_low
            for part in range(atoms // 16):
                piece[atoms + CHANNELS :, part * ATOM_LEN : (part + 1) * ATOM_LEN] = kept[
                    pl.ds(pl.multiple_of(first + part * 16, 16), 16), 0:ATOM_LEN
                ]
            piece[atoms + CHANNELS :, HALO : HALO + ATOM_LEN] = tail
            piece[atoms + CHANNELS :, HALO + ATOM_LEN :] = jnp.zeros(
                (16, width - HALO - ATOM_LEN), BF16
            )
    else:
        outs[1][...] = ahead
        outs[2][...] = resid_low
        outs[3][...] = jnp.full((8, 128), loss, F32)


def correlate(codes_of, resid_of, blocks, atoms, width, stack, pairs, windows):
    main = blocks * width
    length = width + ATOM_LEN
    lane = lax.broadcasted_iota(jnp.int32, (atoms, ATOM_LEN), 1)
    extra = [jnp.zeros((atoms, ATOM_LEN), F32) for _ in range(COARSE)]
    windows[main : main + ATOM_LEN, :] = jnp.zeros((ATOM_LEN, WIDE), BF16)
    for block in range(blocks):
        piece = jnp.concatenate(
            [resid_of(block).astype(F32), jnp.zeros((CHANNELS, ATOM_LEN), F32)], 1
        )
        piece = pltpu.roll(piece, FINE, 1)
        both = jnp.concatenate([piece, pltpu.roll(piece, length - 1, 1)], 0)
        slot = pairs.at[block % 2]
        slot[...] = both.T
        for step in range(FINE // 2):
            lanes = slice(step * 128, (step + 1) * 128)
            low = 2 * step
            windows[main + block * FINE : main + (block + 1) * FINE, lanes] = slot[
                low : low + FINE, :
            ].astype(BF16)
            low += FINE
            windows[block * width : (block + 1) * width, lanes] = slot[
                low : low + width, :
            ].astype(BF16)
        held = codes_of(block).astype(F32)
        for coarse in range(COARSE):
            start = ATOM_LEN - coarse * FINE
            turned = pltpu.roll(held, length - start, 1)
            stack[coarse * atoms : (coarse + 1) * atoms, block * width : (block + 1) * width] = (
                turned[:, :width].astype(BF16)
            )
            turned = pltpu.roll(held, (FINE * block - (start - FINE)) % length, 1)[:, :ATOM_LEN]
            inside = (lane >= FINE * block) & (lane < FINE * (block + 1))
            extra[coarse] = jnp.where(inside, turned, extra[coarse])
    for coarse in range(COARSE):
        stack[coarse * atoms : (coarse + 1) * atoms, main : main + ATOM_LEN] = extra[coarse].astype(
            BF16
        )
    return jnp.dot(stack[...], windows[...], preferred_element_type=F32)


def shared_part(pieces, stack, pairs, windows):
    rows, width = pieces[0].shape
    atoms = rows - CHANNELS - 16

    def codes_of(block):
        before = [
            pieces[block][atoms + CHANNELS :, part * ATOM_LEN : (part + 1) * ATOM_LEN]
            for part in range(atoms // 16)
        ]
        return jnp.concatenate(
            [jnp.concatenate(before, 0).astype(F32), pieces[block][0:atoms, :].astype(F32)], 1
        )

    def resid_of(block):
        return pieces[block][atoms : atoms + CHANNELS, :]

    loss = jnp.zeros((16, ATOM_LEN), F32)
    for piece in pieces:
        loss += piece[atoms + CHANNELS :, HALO : HALO + ATOM_LEN].astype(F32)
    lane = lax.broadcasted_iota(jnp.int32, (16, ATOM_LEN), 1)
    loss = jnp.sum(jnp.where(lane < 3, loss, 0.0), 1, keepdims=True)[0:8]
    total = correlate(
        codes_of, resid_of, len(pieces), atoms, width, stack, pairs, windows
    )
    return total, jnp.broadcast_to(loss, (8, WIDE))


def shared_first(*refs):
    pieces, (out, stack, pairs, windows) = refs[: PEERS // 2], refs[PEERS // 2 :]
    total, loss = shared_part(pieces, stack, pairs, windows)
    rows = total.shape[0]
    out[0:rows, :] = total
    out[rows:, :] = loss


def shared_second(core, before, *refs):
    pieces, (keep, give, stack, pairs, windows, total) = refs[: PEERS // 2], refs[PEERS // 2 :]
    sums, loss = shared_part(pieces, stack, pairs, windows)
    rows = total.shape[0]
    atoms = rows // COARSE
    total[...] = sums + before[0:rows, :]
    half = atoms // 2
    mine = core[0] * half
    other = half - mine
    for coarse in range(COARSE):
        rows_of = slice(coarse * half, (coarse + 1) * half)
        keep[rows_of, :] = total[pl.ds(coarse * atoms + mine, half), :]
        give[rows_of, :] = total[pl.ds(coarse * atoms + other, half), :]
    ending = loss + before[rows:, :]
    keep[COARSE * half :, :] = ending
    give[COARSE * half :, :] = ending


def lone_kernel(codes, resid, out, stack, pairs, windows):
    out[...] = correlate(
        lambda b: codes[...], lambda b: resid[...], 1, ATOMS, resid.shape[1], stack, pairs, windows
    )


def last_kernel(inverse, keep, recv_any, atoms_ref, out, loss_out, total, turned, recv, sem):
    copy = pltpu.make_async_copy(recv_any, recv, sem.at[0])
    copy.start()
    copy.wait()
    half = atoms_ref.shape[0]
    loss_out[0] = (keep[COARSE * half, 0] + recv[COARSE * half, 0]) * inverse
    for step in range(FINE // 2):
        lanes = slice(step * 128, (step + 1) * 128)
        total[step] = keep[0 : COARSE * half, lanes] + recv[0 : COARSE * half, lanes]
    for pair in range(half // 2):
        for step in range(FINE // 2):
            one = total.at[step][pl.ds(2 * pair, COARSE, stride=half), :]
            two = total.at[step][pl.ds(2 * pair + 1, COARSE, stride=half), :]
            block = turned.at[pair]
            block[pl.ds(2 * step, COARSE, stride=FINE), :] = jnp.concatenate(
                [one[:, 0:64], two[:, 0:64]], 1
            )
            block[pl.ds(2 * step + 1, COARSE, stride=FINE), :] = jnp.concatenate(
                [one[:, 64:128], two[:, 64:128]], 1
            )
    gradient = jnp.concatenate([turned[pair].T for pair in range(half // 2)], 0)
    gradient = gradient.reshape(half, CHANNELS, ATOM_LEN)
    normed = gradient / jnp.sqrt(
        jnp.mean(gradient * gradient, axis=(1, 2), keepdims=True) + EPSILON
    )
    moved = atoms_ref[...].astype(F32) - DICT_RATE * normed
    out[...] = moved / jnp.sqrt(jnp.mean(moved * moved, axis=(1, 2), keepdims=True) + EPSILON)


def body(signal, dictionary, step):
    width = signal.shape[1]
    count = lax.axis_size("tm")
    me = lax.axis_index("tm")
    left = shifted(signal[:, width - HALO :], "tm", 1)
    right = shifted(signal[:, :HALO], "tm", -1)
    lags = jnp.transpose(dictionary, (2, 1, 0)).reshape(ATOM_LEN * CHANNELS, ATOMS)
    rows1 = width + 3 * ATOM_LEN
    span = width + 2 * HALO

    near_scratch = [pltpu.VMEM((CHANNELS, HALO), F32)]
    sems = [pltpu.SemaphoreType.DMA((COARSE + 2,))]
    bordered = width + ATOM_LEN
    gradient, peak = pl.pallas_call(
        own_kernel,
        out_shape=(
            jax.ShapeDtypeStruct((width, ATOMS), F32),
            jax.ShapeDtypeStruct((count, 8, 128), F32),
        ),
        in_specs=[vmem(), anywhere(), vmem()],
        out_specs=(vmem(),) * 2,
        scratch_shapes=near_scratch
        + [pltpu.VMEM((bordered, 128), F32), pltpu.VMEM((bordered, WIDE), BF16)]
        + sems,
        compiler_params=kernel_params(),
        cost_estimate=cost(2 * width * ATOMS * WIDE * COARSE, 5 << 20),
    )(signal, right, lags)
    peak = lax.all_to_all(peak, "tm", 0, 0, tiled=False)
    span_border = 2 * HALO + ATOM_LEN
    border, lags = pl.pallas_call(
        border_kernel,
        out_shape=(
            jax.ShapeDtypeStruct((HALO + ATOM_LEN, ATOMS), F32),
            jax.ShapeDtypeStruct(lags.shape, BF16),
        ),
        in_specs=[anywhere(), vmem(), anywhere(), vmem()],
        out_specs=(vmem(), vmem()),
        scratch_shapes=near_scratch * 2
        + [pltpu.VMEM((span_border, 128), F32), pltpu.VMEM((span_border, WIDE), BF16)]
        + sems,
        compiler_params=kernel_params(),
        cost_estimate=cost(2 * (HALO + ATOM_LEN) * ATOMS * WIDE * COARSE, 5 << 20),
    )(left, signal, right, lags)

    valid = jnp.stack(
        [jnp.where(me == 0, HALO, 0), jnp.where(me == count - 1, HALO + width, span)]
        + [(me // 2) ^ turn for turn in range(PEERS)]
    ).astype(jnp.int32)
    owned = ATOMS // count
    shared = count == 2 * PEERS
    own_atoms = lax.dynamic_slice_in_dim(dictionary, me * owned, owned, 0)
    if shared:
        rows = ATOMS // PEERS + CHANNELS + 16
        outs = (jax.ShapeDtypeStruct((rows, width), BF16),) * PEERS
    else:
        outs = (
            jax.ShapeDtypeStruct((ATOMS, width + ATOM_LEN), BF16),
            jax.ShapeDtypeStruct((CHANNELS, width), BF16),
            jax.ShapeDtypeStruct((8, 128), F32),
        )
    codes, *others = pl.pallas_call(
        second_kernel,
        out_shape=(jax.ShapeDtypeStruct((ATOMS, width), F32),) + outs,
        in_specs=[anywhere(), vmem(), anywhere(), vmem()] + [vmem()] * 3 + [smem()] * 2,
        out_specs=(vmem(),) * (1 + len(outs)),
        scratch_shapes=[
            pltpu.VMEM((span, CHANNELS), F32),
            pltpu.VMEM((rows1, ATOMS), F32),
            pltpu.VMEM((rows1, ATOMS), BF16),
            pltpu.VMEM((rows1, 128), F32),
            pltpu.VMEM((rows1, WIDE), BF16),
            pltpu.VMEM((rows1, COARSE * ATOMS), BF16),
            pltpu.VMEM((rows1, WIDE), F32),
            pltpu.VMEM((rows1, 128), F32),
        ]
        + near_scratch * 2
        + sems
        + [pltpu.VMEM((ATOMS, width + ATOM_LEN), BF16)],
        compiler_params=kernel_params(),
    )(left, signal, right, lags, gradient, border, peak, step, valid)

    def correlate_scratch(blocks, atoms):
        return [
            pltpu.VMEM((COARSE * atoms, blocks * width + ATOM_LEN), BF16),
            pltpu.VMEM((2, width + ATOM_LEN, 128), F32),
            pltpu.VMEM((blocks * width + ATOM_LEN, WIDE), BF16),
        ]

    inverse = 1.0 / (CHANNELS * width * count)
    if shared:
        core = me % 2
        pieces = list(others)
        for turn in (4, 5, 6, 7, 2, 3, 1):
            pieces[turn] = swapped(pieces[turn], 2 * turn)
        half_rows = jax.ShapeDtypeStruct((COARSE * owned + 8, WIDE), F32)
        blocks = PEERS // 2
        before = pl.pallas_call(
            shared_first,
            out_shape=jax.ShapeDtypeStruct((COARSE * 2 * owned + 8, WIDE), F32),
            in_specs=[vmem()] * blocks,
            out_specs=vmem(),
            scratch_shapes=correlate_scratch(blocks, 2 * owned),
            compiler_params=kernel_params(),
            cost_estimate=cost(2 * COARSE * 2 * owned * blocks * width * WIDE, 2 << 20),
        )(*pieces[:blocks])
        keep, give = pl.pallas_call(
            shared_second,
            out_shape=(half_rows, half_rows),
            in_specs=[smem(), vmem()] + [vmem()] * blocks,
            out_specs=(vmem(), vmem()),
            scratch_shapes=correlate_scratch(blocks, 2 * owned)
            + [pltpu.VMEM((COARSE * 2 * owned, WIDE), F32)],
            compiler_params=kernel_params(),
            cost_estimate=cost(2 * COARSE * 2 * owned * blocks * width * WIDE, 2 << 20),
        )(core.reshape(1).astype(jnp.int32), before, *pieces[blocks:])
        recv = swapped(give, 1)
        new_dictionary, loss = pl.pallas_call(
            lambda *refs: last_kernel(inverse, *refs),
            out_shape=(
                jax.ShapeDtypeStruct((owned, CHANNELS, ATOM_LEN), F32),
                jax.ShapeDtypeStruct((1,), F32),
            ),
            in_specs=[vmem(), anywhere(), vmem()],
            out_specs=(vmem(), smem()),
            scratch_shapes=[
                pltpu.VMEM((FINE // 2, COARSE * owned, 128), F32),
                pltpu.VMEM((owned // 2, ATOM_LEN, 2 * CHANNELS), F32),
                pltpu.VMEM(half_rows.shape, F32),
                pltpu.SemaphoreType.DMA((1,)),
            ],
            compiler_params=kernel_params(),
        )(keep, recv, own_atoms)
        return (codes, new_dictionary, loss)

    ahead, resid, loss = others
    part = pl.pallas_call(
        lone_kernel,
        out_shape=jax.ShapeDtypeStruct((COARSE * ATOMS, WIDE), F32),
        in_specs=[vmem()] * 2,
        out_specs=vmem(),
        scratch_shapes=correlate_scratch(1, ATOMS),
        compiler_params=kernel_params(),
    )(ahead, resid)
    summed = lax.psum_scatter(
        part.reshape(COARSE, ATOMS, WIDE), "tm", scatter_dimension=1, tiled=True
    )
    atom_gradient = (
        summed.reshape(COARSE, owned, FINE, CHANNELS)
        .transpose(1, 3, 0, 2)
        .reshape(owned, CHANNELS, ATOM_LEN)
    )
    normed = atom_gradient / jnp.sqrt(
        jnp.mean(atom_gradient * atom_gradient, axis=(1, 2), keepdims=True) + EPSILON
    )
    moved = own_atoms.astype(F32) - DICT_RATE * normed
    new_dictionary = moved / jnp.sqrt(
        jnp.mean(moved * moved, axis=(1, 2), keepdims=True) + EPSILON
    )
    bit = 1
    while bit < count:
        loss = loss + swapped(loss, bit)
        bit *= 2
    return (codes, new_dictionary, loss[0, :1] * inverse)


def solution(mesh):
    return jax.shard_map(
        body,
        mesh=mesh,
        in_specs=(P(None, ("groups", "tm")), P(), P()),
        out_specs=(P(None, ("groups", "tm")), P(("groups", "tm"), None, None), P("groups")),
        check_vma=False,
    )
```

```python
import math

import jax
import jax.numpy as jnp
from jax import lax
from jax.experimental import pallas as pl
from jax.experimental.pallas import tpu as pltpu
from jax.sharding import PartitionSpec as P

ATOMS = 256
CHANNELS = 64
ATOM_LEN = 128
SPARSITY = 0.05
DICT_RATE = 0.5
EPSILON = 1e-06

SCALE = 1.0 / math.sqrt(CHANNELS * ATOM_LEN)
FINE = 16
COARSE = ATOM_LEN // FINE
WIDE = FINE * CHANNELS
HALO = 2 * ATOM_LEN
F32 = jnp.float32
BF16 = jnp.bfloat16
PITCH = CHANNELS + 8
PEERS = 8
OWN_LIMIT = 60 * 1024 * 1024
VMEM_LIMIT = 36 * 1024 * 1024


def vmem():
    return pl.BlockSpec(memory_space=pltpu.VMEM)


def smem():
    return pl.BlockSpec(memory_space=pltpu.SMEM)


def anywhere():
    return pl.BlockSpec(memory_space=pl.ANY)


def fetch_lags(source, lags, arrived):
    copies = [
        pltpu.make_async_copy(
            source.at[pl.ds(coarse * WIDE, WIDE), :],
            lags.at[pl.ds(coarse * WIDE, WIDE), :],
            arrived.at[coarse],
        )
        for coarse in range(COARSE)
    ]
    for copy in copies:
        copy.start()
    return copies


def cost(flops, bytes_accessed):
    return pl.CostEstimate(flops=flops, bytes_accessed=bytes_accessed, transcendentals=0)


def kernel_params(limit=VMEM_LIMIT):
    return pltpu.CompilerParams(vmem_limit_bytes=limit)


def shifted(value, axis, steps):
    count = lax.axis_size(axis)
    leading, last = (max(0, -steps), min(count, count - steps))
    return lax.ppermute(value, axis, [(source, source + steps) for source in range(leading, last)])


def swapped(value, bit):
    count = lax.axis_size("tm")
    return lax.ppermute(value, "tm", [(i, i ^ bit) for i in range(count)])


def fill_windows(pairs, windows, rows):
    for step in range(FINE // 2):
        windows[0:rows, step * 128 : (step + 1) * 128] = pairs[
            2 * step : 2 * step + rows, :
        ].astype(BF16)


def adjoint(windows, lags, total, spans, copies=None):
    rows = sum(count for _, count in spans)
    for coarse in range(COARSE):
        if copies is not None:
            copies[coarse].wait()
        shift = coarse * FINE
        taken = [windows[start + shift : start + shift + count, :] for start, count in spans]
        part = jnp.dot(
            taken[0] if len(taken) == 1 else jnp.concatenate(taken, 0),
            lags[coarse * WIDE : (coarse + 1) * WIDE, :],
            preferred_element_type=F32,
        )
        if coarse == 0:
            total[0:rows, :] = part
        else:
            total[0:rows, :] += part


def windows_of(whole, pairs, windows):
    length = whole.shape[1]
    both = jnp.concatenate([whole, pltpu.roll(whole, length - 1, 1)], 0)
    pairs[0:length, :] = both.T
    fill_windows(pairs, windows, length - FINE)


def turn_dictionary(atoms, lags, by_atom, by_lag, copies):
    half = ATOMS // 2
    for part in range(2):
        copies[part].wait()
        for atom in range(half):
            by_atom[atom * PITCH : atom * PITCH + CHANNELS, :] = atoms[part * half + atom].astype(
                F32
            )
        for channel in range(CHANNELS):
            turned = by_atom[pl.ds(channel, half, stride=PITCH), :].T
            by_lag[pl.ds(channel, ATOM_LEN, stride=PITCH), :] = turned
        for lag in range(ATOM_LEN):
            lags[lag * CHANNELS : (lag + 1) * CHANNELS, part * half : (part + 1) * half] = by_lag[
                lag * PITCH : lag * PITCH + CHANNELS, :
            ].astype(BF16)


def own_kernel(
    middle, right_any, atoms_any, gradient, largest, lags_out,
    right, atoms, lags, by_atom, by_lag, pairs, windows, sems, atom_sems,
):
    width = middle.shape[1]
    half = ATOMS // 2
    loads = [
        pltpu.make_async_copy(
            atoms_any.at[pl.ds(part * half, half)],
            atoms.at[pl.ds(part * half, half)],
            atom_sems.at[part],
        )
        for part in range(2)
    ]
    loads[0].start()
    near = pltpu.make_async_copy(right_any.at[:, pl.ds(0, HALO)], right, sems.at[COARSE])
    near.start()
    loads[1].start()
    near.wait()
    whole = jnp.concatenate([middle[...], right[:, 0:ATOM_LEN]], 1)
    windows_of(-whole, pairs, windows)
    turn_dictionary(atoms, lags, by_atom, by_lag, loads)
    copies = fetch_lags(lags, lags_out, sems)
    adjoint(windows, lags, gradient, [(0, width)])
    own = jnp.abs(gradient[...]) * SCALE
    folded = jnp.max(own.reshape(width // 8, 8, ATOMS), 0)
    folded = jnp.maximum(folded[:, :128], folded[:, 128:])
    for peer in range(largest.shape[0]):
        largest[peer] = folded
    for copy in copies:
        copy.wait()


def border_kernel(
    left_any, middle, right_any, lags, gradient, left, right, pairs, windows, sems
):
    near = [
        pltpu.make_async_copy(
            left_any.at[:, pl.ds(left_any.shape[1] - HALO, HALO)], left, sems.at[COARSE]),
        pltpu.make_async_copy(right_any.at[:, pl.ds(0, HALO)], right, sems.at[COARSE + 1]),
    ]
    for copy in near:
        copy.start()
    for copy in near:
        copy.wait()
    whole = jnp.concatenate([left[...], middle[:, 0:ATOM_LEN], right[...]], 1)
    windows_of(-whole, pairs, windows)
    adjoint(windows, lags, gradient, [(0, HALO), (HALO + ATOM_LEN, ATOM_LEN)])


def forward(codes, lags, wide, spread, folded, start, rows):
    for coarse in range(COARSE):
        low = start - coarse * FINE
        wide[0:rows, coarse * ATOMS : (coarse + 1) * ATOMS] = codes[low : low + rows, :]
    weights = jnp.concatenate(
        [lags[coarse * WIDE : (coarse + 1) * WIDE, :] for coarse in range(COARSE)], 1
    )
    spread[0:rows, :] = lax.dot_general(
        wide[0:rows, :], weights, (((1,), (1,)), ((), ())), preferred_element_type=F32
    )
    keep = rows - FINE
    total = spread[FINE - 2 : FINE - 2 + keep + 2, 0:128]
    for step in range(1, FINE // 2):
        lanes = slice(step * 128, (step + 1) * 128)
        low = FINE - 2 - 2 * step
        total = total + spread[low : low + keep + 2, lanes]
    folded[0 : keep + 2, :] = total
    return folded[2 : keep + 2, 0:64] + folded[1 : keep + 1, 64:128]


def soft(moved, bound):
    return jnp.where(moved > 0, 1.0, -1.0) * jnp.maximum(jnp.abs(moved) - bound, 0.0)


def second_kernel(
    left_any, middle, right_any, lags, own_gradient, border, peak, step, valid, *rest
):
    outs, scratch, kept = rest[:-12], rest[-12:-1], rest[-1]
    signal, codes, codes_low, pairs, windows, wide, spread, folded = scratch[:8]
    left, right, sems = scratch[8:]
    near = [
        pltpu.make_async_copy(
            left_any.at[:, pl.ds(left_any.shape[1] - HALO, HALO)], left, sems.at[COARSE]),
        pltpu.make_async_copy(right_any.at[:, pl.ds(0, HALO)], right, sems.at[COARSE + 1]),
    ]
    for copy in near:
        copy.start()
    for copy in near:
        copy.wait()
    width = middle.shape[1]
    step_size = step[0]
    threshold = SPARSITY * jnp.max(peak[...])
    bound = step_size * threshold
    low, high = valid[0], valid[1]
    whole = jnp.concatenate([left[...], middle[...], right[...]], 1)
    signal[...] = whole.T

    def row(start, count):
        return lax.broadcasted_iota(jnp.int32, (count, 1), 0) + start

    for start, values in (
        (0, border[0:HALO, :]),
        (HALO, own_gradient[...]),
        (HALO + width, border[HALO:, :]),
    ):
        count = values.shape[0]
        moved = -step_size * (values * SCALE)
        updated = soft(moved, bound)
        if start == 0:
            updated = jnp.where(row(0, count) >= low, updated, 0.0)
        codes[start : start + count, :] = updated
        codes_low[start : start + count, :] = updated.astype(BF16)
    rows2 = width + 2 * ATOM_LEN
    model = forward(codes_low, lags, wide, spread, folded, ATOM_LEN - FINE, rows2 + FINE)
    resid = model * SCALE - signal[ATOM_LEN : ATOM_LEN + rows2, :]
    resid = jnp.where(row(ATOM_LEN, rows2) < high, resid, 0.0)
    pairs[0:rows2, 0:64] = resid
    pairs[0 : rows2 - 1, 64:128] = pairs[1:rows2, 0:64]
    fill_windows(pairs, windows, rows2 - FINE)
    rows3 = width + ATOM_LEN
    adjoint(windows, lags, spread.at[:, 0:ATOMS], [(0, rows3)])
    before = codes[ATOM_LEN : ATOM_LEN + rows3, :]
    moved = before - step_size * (spread[0:rows3, 0:ATOMS] * SCALE)
    updated = jnp.where(row(ATOM_LEN, rows3) >= low, soft(moved, bound), 0.0)
    codes[0:rows3, :] = updated
    codes_low[0:rows3, :] = updated.astype(BF16)
    turned = updated.T
    outs[0][...] = turned[:, ATOM_LEN:]
    sparse = jnp.sum(jnp.abs(codes[ATOM_LEN:rows3, :]))
    model = forward(codes_low, lags, wide, spread, folded, ATOM_LEN - FINE, width + FINE)
    resid = model * SCALE - signal[HALO : HALO + width, :]
    resid_low = resid.T.astype(BF16)
    ahead = turned.astype(BF16)
    loss = 0.5 * jnp.sum(resid * resid) + threshold * sparse
    if len(outs) == 1 + PEERS:
        atoms = ATOMS // PEERS
        whole_loss = jnp.full((16, ATOM_LEN), loss, F32)
        high_part = whole_loss.astype(BF16)
        rest_loss = whole_loss - high_part.astype(F32)
        middle_part = rest_loss.astype(BF16)
        low_part = (rest_loss - middle_part.astype(F32)).astype(BF16)
        lane = lax.broadcasted_iota(jnp.int32, (16, ATOM_LEN), 1)
        tail = jnp.where(
            lane == 0,
            high_part.astype(F32),
            jnp.where(lane == 1, middle_part.astype(F32), low_part.astype(F32)),
        ).astype(BF16)
        kept[...] = ahead
        for turn in range(PEERS):
            first = pl.multiple_of(valid[2 + turn] * atoms, atoms)
            piece = outs[1 + turn]
            piece[0:atoms, :] = kept[pl.ds(first, atoms), ATOM_LEN:]
            piece[atoms : atoms + CHANNELS, :] = resid_low
            for part in range(atoms // 16):
                piece[atoms + CHANNELS :, part * ATOM_LEN : (part + 1) * ATOM_LEN] = kept[
                    pl.ds(pl.multiple_of(first + part * 16, 16), 16), 0:ATOM_LEN
                ]
            piece[atoms + CHANNELS :, HALO : HALO + ATOM_LEN] = tail
            piece[atoms + CHANNELS :, HALO + ATOM_LEN :] = jnp.zeros(
                (16, width - HALO - ATOM_LEN), BF16
            )
    else:
        outs[1][...] = ahead
        outs[2][...] = resid_low
        outs[3][...] = jnp.full((8, 128), loss, F32)


def correlate(codes_of, resid_of, blocks, atoms, width, stack, pairs, windows):
    main = blocks * width
    length = width + ATOM_LEN
    lane = lax.broadcasted_iota(jnp.int32, (atoms, ATOM_LEN), 1)
    extra = [jnp.zeros((atoms, ATOM_LEN), F32) for _ in range(COARSE)]
    windows[main : main + ATOM_LEN, :] = jnp.zeros((ATOM_LEN, WIDE), BF16)
    for block in range(blocks):
        piece = jnp.concatenate(
            [resid_of(block).astype(F32), jnp.zeros((CHANNELS, ATOM_LEN), F32)], 1
        )
        piece = pltpu.roll(piece, FINE, 1)
        both = jnp.concatenate([piece, pltpu.roll(piece, length - 1, 1)], 0)
        slot = pairs.at[block % 2]
        slot[...] = both.T
        for step in range(FINE // 2):
            lanes = slice(step * 128, (step + 1) * 128)
            low = 2 * step
            windows[main + block * FINE : main + (block + 1) * FINE, lanes] = slot[
                low : low + FINE, :
            ].astype(BF16)
            low += FINE
            windows[block * width : (block + 1) * width, lanes] = slot[
                low : low + width, :
            ].astype(BF16)
        held = codes_of(block).astype(F32)
        for coarse in range(COARSE):
            start = ATOM_LEN - coarse * FINE
            turned = pltpu.roll(held, length - start, 1)
            stack[coarse * atoms : (coarse + 1) * atoms, block * width : (block + 1) * width] = (
                turned[:, :width].astype(BF16)
            )
            turned = pltpu.roll(held, (FINE * block - (start - FINE)) % length, 1)[:, :ATOM_LEN]
            inside = (lane >= FINE * block) & (lane < FINE * (block + 1))
            extra[coarse] = jnp.where(inside, turned, extra[coarse])
    for coarse in range(COARSE):
        stack[coarse * atoms : (coarse + 1) * atoms, main : main + ATOM_LEN] = extra[coarse].astype(
            BF16
        )
    return jnp.dot(stack[...], windows[...], preferred_element_type=F32)


def shared_part(pieces, stack, pairs, windows):
    rows, width = pieces[0].shape
    atoms = rows - CHANNELS - 16

    def codes_of(block):
        before = [
            pieces[block][atoms + CHANNELS :, part * ATOM_LEN : (part + 1) * ATOM_LEN]
            for part in range(atoms // 16)
        ]
        return jnp.concatenate(
            [jnp.concatenate(before, 0).astype(F32), pieces[block][0:atoms, :].astype(F32)], 1
        )

    def resid_of(block):
        return pieces[block][atoms : atoms + CHANNELS, :]

    loss = jnp.zeros((16, ATOM_LEN), F32)
    for piece in pieces:
        loss += piece[atoms + CHANNELS :, HALO : HALO + ATOM_LEN].astype(F32)
    lane = lax.broadcasted_iota(jnp.int32, (16, ATOM_LEN), 1)
    loss = jnp.sum(jnp.where(lane < 3, loss, 0.0), 1, keepdims=True)[0:8]
    total = correlate(
        codes_of, resid_of, len(pieces), atoms, width, stack, pairs, windows
    )
    return total, jnp.broadcast_to(loss, (8, WIDE))


def shared_first(*refs):
    pieces, (out, stack, pairs, windows) = refs[: PEERS // 2], refs[PEERS // 2 :]
    total, loss = shared_part(pieces, stack, pairs, windows)
    rows = total.shape[0]
    out[0:rows, :] = total
    out[rows:, :] = loss


def shared_second(core, before, *refs):
    pieces, (keep, give, stack, pairs, windows, total) = refs[: PEERS // 2], refs[PEERS // 2 :]
    sums, loss = shared_part(pieces, stack, pairs, windows)
    rows = total.shape[0]
    atoms = rows // COARSE
    total[...] = sums + before[0:rows, :]
    half = atoms // 2
    mine = core[0] * half
    other = half - mine
    for coarse in range(COARSE):
        rows_of = slice(coarse * half, (coarse + 1) * half)
        keep[rows_of, :] = total[pl.ds(coarse * atoms + mine, half), :]
        give[rows_of, :] = total[pl.ds(coarse * atoms + other, half), :]
    ending = loss + before[rows:, :]
    keep[COARSE * half :, :] = ending
    give[COARSE * half :, :] = ending


def lone_kernel(codes, resid, out, stack, pairs, windows):
    out[...] = correlate(
        lambda b: codes[...], lambda b: resid[...], 1, ATOMS, resid.shape[1], stack, pairs, windows
    )


def last_kernel(inverse, keep, recv_any, atoms_ref, out, loss_out, total, turned, recv, sem):
    copy = pltpu.make_async_copy(recv_any, recv, sem.at[0])
    copy.start()
    copy.wait()
    half = atoms_ref.shape[0]
    loss_out[0] = (keep[COARSE * half, 0] + recv[COARSE * half, 0]) * inverse
    for step in range(FINE // 2):
        lanes = slice(step * 128, (step + 1) * 128)
        total[step] = keep[0 : COARSE * half, lanes] + recv[0 : COARSE * half, lanes]
    for pair in range(half // 2):
        for step in range(FINE // 2):
            one = total.at[step][pl.ds(2 * pair, COARSE, stride=half), :]
            two = total.at[step][pl.ds(2 * pair + 1, COARSE, stride=half), :]
            block = turned.at[pair]
            block[pl.ds(2 * step, COARSE, stride=FINE), :] = jnp.concatenate(
                [one[:, 0:64], two[:, 0:64]], 1
            )
            block[pl.ds(2 * step + 1, COARSE, stride=FINE), :] = jnp.concatenate(
                [one[:, 64:128], two[:, 64:128]], 1
            )
    gradient = jnp.concatenate([turned[pair].T for pair in range(half // 2)], 0)
    gradient = gradient.reshape(half, CHANNELS, ATOM_LEN)
    normed = gradient / jnp.sqrt(
        jnp.mean(gradient * gradient, axis=(1, 2), keepdims=True) + EPSILON
    )
    moved = atoms_ref[...].astype(F32) - DICT_RATE * normed
    out[...] = moved / jnp.sqrt(jnp.mean(moved * moved, axis=(1, 2), keepdims=True) + EPSILON)


def body(signal, dictionary, step):
    width = signal.shape[1]
    count = lax.axis_size("tm")
    me = lax.axis_index("tm")
    left = shifted(signal, "tm", 1)
    right = shifted(signal, "tm", -1)
    rows1 = width + 3 * ATOM_LEN
    span = width + 2 * HALO

    near_scratch = [pltpu.VMEM((CHANNELS, HALO), F32)]
    sems = [pltpu.SemaphoreType.DMA((COARSE + 2,))]
    bordered = width + ATOM_LEN
    gradient, peak, lags = pl.pallas_call(
        own_kernel,
        out_shape=(
            jax.ShapeDtypeStruct((width, ATOMS), F32),
            jax.ShapeDtypeStruct((count, 8, 128), F32),
            jax.ShapeDtypeStruct((ATOM_LEN * CHANNELS, ATOMS), BF16),
        ),
        in_specs=[vmem(), anywhere(), pl.BlockSpec(memory_space=pltpu.HBM)],
        out_specs=(vmem(), vmem(), pl.BlockSpec(memory_space=pltpu.HBM)),
        scratch_shapes=near_scratch
        + [pltpu.VMEM(dictionary.shape, BF16)]
        + [pltpu.VMEM((ATOM_LEN * CHANNELS, ATOMS), BF16)]
        + [pltpu.VMEM((ATOM_LEN * PITCH, 128), F32)] * 2
        + [pltpu.VMEM((bordered, 128), F32), pltpu.VMEM((bordered, WIDE), BF16)]
        + sems
        + [pltpu.SemaphoreType.DMA((2,))],
        compiler_params=kernel_params(OWN_LIMIT),
        cost_estimate=cost(2 * width * ATOMS * WIDE * COARSE, 5 << 20),
    )(signal, right, dictionary)
    peak = lax.all_to_all(peak, "tm", 0, 0, tiled=False)
    span_border = 2 * HALO + ATOM_LEN
    border = pl.pallas_call(
        border_kernel,
        out_shape=jax.ShapeDtypeStruct((HALO + ATOM_LEN, ATOMS), F32),
        in_specs=[anywhere(), vmem(), anywhere(), vmem()],
        out_specs=vmem(),
        scratch_shapes=near_scratch * 2
        + [pltpu.VMEM((span_border, 128), F32), pltpu.VMEM((span_border, WIDE), BF16)]
        + sems,
        compiler_params=kernel_params(),
        cost_estimate=cost(2 * (HALO + ATOM_LEN) * ATOMS * WIDE * COARSE, 5 << 20),
    )(left, signal, right, lags)

    valid = jnp.stack(
        [jnp.where(me == 0, HALO, 0), jnp.where(me == count - 1, HALO + width, span)]
        + [(me // 2) ^ turn for turn in range(PEERS)]
    ).astype(jnp.int32)
    owned = ATOMS // count
    shared = count == 2 * PEERS
    own_atoms = lax.dynamic_slice_in_dim(dictionary, me * owned, owned, 0)
    if shared:
        rows = ATOMS // PEERS + CHANNELS + 16
        outs = (jax.ShapeDtypeStruct((rows, width), BF16),) * PEERS
    else:
        outs = (
            jax.ShapeDtypeStruct((ATOMS, width + ATOM_LEN), BF16),
            jax.ShapeDtypeStruct((CHANNELS, width), BF16),
            jax.ShapeDtypeStruct((8, 128), F32),
        )
    codes, *others = pl.pallas_call(
        second_kernel,
        out_shape=(jax.ShapeDtypeStruct((ATOMS, width), F32),) + outs,
        in_specs=[anywhere(), vmem(), anywhere(), vmem()] + [vmem()] * 3 + [smem()] * 2,
        out_specs=(vmem(),) * (1 + len(outs)),
        scratch_shapes=[
            pltpu.VMEM((span, CHANNELS), F32),
            pltpu.VMEM((rows1, ATOMS), F32),
            pltpu.VMEM((rows1, ATOMS), BF16),
            pltpu.VMEM((rows1, 128), F32),
            pltpu.VMEM((rows1, WIDE), BF16),
            pltpu.VMEM((rows1, COARSE * ATOMS), BF16),
            pltpu.VMEM((rows1, WIDE), F32),
            pltpu.VMEM((rows1, 128), F32),
        ]
        + near_scratch * 2
        + sems
        + [pltpu.VMEM((ATOMS, width + ATOM_LEN), BF16)],
        compiler_params=kernel_params(),
    )(left, signal, right, lags, gradient, border, peak, step, valid)

    def correlate_scratch(blocks, atoms):
        return [
            pltpu.VMEM((COARSE * atoms, blocks * width + ATOM_LEN), BF16),
            pltpu.VMEM((2, width + ATOM_LEN, 128), F32),
            pltpu.VMEM((blocks * width + ATOM_LEN, WIDE), BF16),
        ]

    inverse = 1.0 / (CHANNELS * width * count)
    if shared:
        core = me % 2
        pieces = list(others)
        for turn in range(1, PEERS):
            pieces[turn] = swapped(pieces[turn], 2 * turn)
        half_rows = jax.ShapeDtypeStruct((COARSE * owned + 8, WIDE), F32)
        blocks = PEERS // 2
        before = pl.pallas_call(
            shared_first,
            out_shape=jax.ShapeDtypeStruct((COARSE * 2 * owned + 8, WIDE), F32),
            in_specs=[vmem()] * blocks,
            out_specs=vmem(),
            scratch_shapes=correlate_scratch(blocks, 2 * owned),
            compiler_params=kernel_params(),
            cost_estimate=cost(2 * COARSE * 2 * owned * blocks * width * WIDE, 2 << 20),
        )(*[pieces[turn] for turn in (0, 4, 5, 6)])
        keep, give = pl.pallas_call(
            shared_second,
            out_shape=(half_rows, half_rows),
            in_specs=[smem(), vmem()] + [vmem()] * blocks,
            out_specs=(vmem(), vmem()),
            scratch_shapes=correlate_scratch(blocks, 2 * owned)
            + [pltpu.VMEM((COARSE * 2 * owned, WIDE), F32)],
            compiler_params=kernel_params(),
            cost_estimate=cost(2 * COARSE * 2 * owned * blocks * width * WIDE, 2 << 20),
        )(core.reshape(1).astype(jnp.int32), before, *[pieces[turn] for turn in (7, 3, 2, 1)])
        recv = swapped(give, 1)
        new_dictionary, loss = pl.pallas_call(
            lambda *refs: last_kernel(inverse, *refs),
            out_shape=(
                jax.ShapeDtypeStruct((owned, CHANNELS, ATOM_LEN), F32),
                jax.ShapeDtypeStruct((1,), F32),
            ),
            in_specs=[vmem(), anywhere(), vmem()],
            out_specs=(vmem(), smem()),
            scratch_shapes=[
                pltpu.VMEM((FINE // 2, COARSE * owned, 128), F32),
                pltpu.VMEM((owned // 2, ATOM_LEN, 2 * CHANNELS), F32),
                pltpu.VMEM(half_rows.shape, F32),
                pltpu.SemaphoreType.DMA((1,)),
            ],
            compiler_params=kernel_params(),
        )(keep, recv, own_atoms)
        return (codes, new_dictionary, loss)

    ahead, resid, loss = others
    part = pl.pallas_call(
        lone_kernel,
        out_shape=jax.ShapeDtypeStruct((COARSE * ATOMS, WIDE), F32),
        in_specs=[vmem()] * 2,
        out_specs=vmem(),
        scratch_shapes=correlate_scratch(1, ATOMS),
        compiler_params=kernel_params(),
    )(ahead, resid)
    summed = lax.psum_scatter(
        part.reshape(COARSE, ATOMS, WIDE), "tm", scatter_dimension=1, tiled=True
    )
    atom_gradient = (
        summed.reshape(COARSE, owned, FINE, CHANNELS)
        .transpose(1, 3, 0, 2)
        .reshape(owned, CHANNELS, ATOM_LEN)
    )
    normed = atom_gradient / jnp.sqrt(
        jnp.mean(atom_gradient * atom_gradient, axis=(1, 2), keepdims=True) + EPSILON
    )
    moved = own_atoms.astype(F32) - DICT_RATE * normed
    new_dictionary = moved / jnp.sqrt(
        jnp.mean(moved * moved, axis=(1, 2), keepdims=True) + EPSILON
    )
    bit = 1
    while bit < count:
        loss = loss + swapped(loss, bit)
        bit *= 2
    return (codes, new_dictionary, loss[0, :1] * inverse)


def solution(mesh):
    return jax.shard_map(
        body,
        mesh=mesh,
        in_specs=(P(None, ("groups", "tm")), P(), P()),
        out_specs=(P(None, ("groups", "tm")), P(("groups", "tm"), None, None), P("groups")),
        check_vma=False,
    )
```

```python
import math

import jax
import jax.numpy as jnp
from jax import lax
from jax.experimental import pallas as pl
from jax.experimental.pallas import tpu as pltpu
from jax.sharding import PartitionSpec as P

ATOMS = 256
CHANNELS = 64
ATOM_LEN = 128
SPARSITY = 0.05
DICT_RATE = 0.5
EPSILON = 1e-06

SCALE = 1.0 / math.sqrt(CHANNELS * ATOM_LEN)
FINE = 16
COARSE = ATOM_LEN // FINE
WIDE = FINE * CHANNELS
HALO = 2 * ATOM_LEN
F32 = jnp.float32
BF16 = jnp.bfloat16
PITCH = CHANNELS + 8
CHUNKS = 2
PEERS = 8
OWN_LIMIT = 60 * 1024 * 1024
VMEM_LIMIT = 36 * 1024 * 1024


def vmem():
    return pl.BlockSpec(memory_space=pltpu.VMEM)


def smem():
    return pl.BlockSpec(memory_space=pltpu.SMEM)


def anywhere():
    return pl.BlockSpec(memory_space=pl.ANY)


def fetch_lags(source, lags, arrived):
    copies = [
        pltpu.make_async_copy(
            source.at[pl.ds(coarse * WIDE, WIDE), :],
            lags.at[pl.ds(coarse * WIDE, WIDE), :],
            arrived.at[coarse],
        )
        for coarse in range(COARSE)
    ]
    for copy in copies:
        copy.start()
    return copies


def cost(flops, bytes_accessed):
    return pl.CostEstimate(flops=flops, bytes_accessed=bytes_accessed, transcendentals=0)


def kernel_params(limit=VMEM_LIMIT):
    return pltpu.CompilerParams(vmem_limit_bytes=limit)


def shifted(value, axis, steps):
    count = lax.axis_size(axis)
    leading, last = (max(0, -steps), min(count, count - steps))
    return lax.ppermute(value, axis, [(source, source + steps) for source in range(leading, last)])


def swapped(value, bit):
    count = lax.axis_size("tm")
    return lax.ppermute(value, "tm", [(i, i ^ bit) for i in range(count)])


def fill_windows(pairs, windows, rows):
    for step in range(FINE // 2):
        windows[0:rows, step * 128 : (step + 1) * 128] = pairs[
            2 * step : 2 * step + rows, :
        ].astype(BF16)


def adjoint(windows, lags, total, spans, copies=None):
    rows = sum(count for _, count in spans)
    for coarse in range(COARSE):
        if copies is not None:
            copies[coarse].wait()
        shift = coarse * FINE
        taken = [windows[start + shift : start + shift + count, :] for start, count in spans]
        part = jnp.dot(
            taken[0] if len(taken) == 1 else jnp.concatenate(taken, 0),
            lags[coarse * WIDE : (coarse + 1) * WIDE, :],
            preferred_element_type=F32,
        )
        if coarse == 0:
            total[0:rows, :] = part
        else:
            total[0:rows, :] += part


def windows_of(whole, pairs, windows):
    length = whole.shape[1]
    both = jnp.concatenate([whole, pltpu.roll(whole, length - 1, 1)], 0)
    pairs[0:length, :] = both.T
    fill_windows(pairs, windows, length - FINE)


def turn_dictionary(atoms, lags, by_atom, by_lag, copies):
    half = ATOMS // 2
    for part in range(2):
        copies[part].wait()
        for atom in range(half):
            by_atom[atom * PITCH : atom * PITCH + CHANNELS, :] = atoms[part * half + atom].astype(
                F32
            )
        for channel in range(CHANNELS):
            turned = by_atom[pl.ds(channel, half, stride=PITCH), :].T
            by_lag[pl.ds(channel, ATOM_LEN, stride=PITCH), :] = turned
        for lag in range(ATOM_LEN):
            lags[lag * CHANNELS : (lag + 1) * CHANNELS, part * half : (part + 1) * half] = by_lag[
                lag * PITCH : lag * PITCH + CHANNELS, :
            ].astype(BF16)


def own_kernel(
    middle, right_any, atoms_any, gradient, largest, lags_out,
    right, atoms, lags, by_atom, by_lag, pairs, windows, sems, atom_sems,
):
    width = middle.shape[1]
    half = ATOMS // 2
    loads = [
        pltpu.make_async_copy(
            atoms_any.at[pl.ds(part * half, half)],
            atoms.at[pl.ds(part * half, half)],
            atom_sems.at[part],
        )
        for part in range(2)
    ]
    loads[0].start()
    near = pltpu.make_async_copy(right_any.at[:, pl.ds(0, HALO)], right, sems.at[COARSE])
    near.start()
    loads[1].start()
    near.wait()
    whole = jnp.concatenate([middle[...], right[:, 0:ATOM_LEN]], 1)
    windows_of(-whole, pairs, windows)
    turn_dictionary(atoms, lags, by_atom, by_lag, loads)
    copies = fetch_lags(lags, lags_out, sems)
    for begin, end in row_chunks(width):
        adjoint(windows, lags, gradient.at[pl.ds(begin, end - begin), :], [(begin, end - begin)])
    own = jnp.abs(gradient[...]) * SCALE
    folded = jnp.max(own.reshape(width // 8, 8, ATOMS), 0)
    folded = jnp.maximum(folded[:, :128], folded[:, 128:])
    for peer in range(largest.shape[0]):
        largest[peer] = folded
    for copy in copies:
        copy.wait()


def border_kernel(
    left_any, middle, right_any, lags, gradient, left, right, pairs, windows, sems
):
    near = [
        pltpu.make_async_copy(
            left_any.at[:, pl.ds(left_any.shape[1] - HALO, HALO)], left, sems.at[COARSE]),
        pltpu.make_async_copy(right_any.at[:, pl.ds(0, HALO)], right, sems.at[COARSE + 1]),
    ]
    for copy in near:
        copy.start()
    for copy in near:
        copy.wait()
    whole = jnp.concatenate([left[...], middle[:, 0:ATOM_LEN], right[...]], 1)
    windows_of(-whole, pairs, windows)
    adjoint(windows, lags, gradient.at[pl.ds(0, HALO), :], [(0, HALO)])
    adjoint(windows, lags, gradient.at[pl.ds(HALO, ATOM_LEN), :], [(HALO + ATOM_LEN, ATOM_LEN)])


def row_chunks(rows):
    size = -(-rows // (CHUNKS * FINE)) * FINE
    return [(low, min(low + size, rows)) for low in range(0, rows, size)]


def forward(codes, lags, wide, spread, folded, start, rows):
    keep = rows - FINE
    weights = jnp.concatenate(
        [lags[coarse * WIDE : (coarse + 1) * WIDE, :] for coarse in range(COARSE)], 1
    )
    done = 0
    for begin, end in row_chunks(rows):
        for coarse in range(COARSE):
            low = start + begin - coarse * FINE
            wide[begin:end, coarse * ATOMS : (coarse + 1) * ATOMS] = codes[
                low : low + end - begin, :
            ]
        spread[begin:end, :] = lax.dot_general(
            wide[begin:end, :], weights, (((1,), (1,)), ((), ())), preferred_element_type=F32
        )
        until = keep + 2 if end == rows else end - FINE
        total = spread[FINE - 2 + done : FINE - 2 + until, 0:128]
        for step in range(1, FINE // 2):
            low = FINE - 2 - 2 * step
            total = total + spread[low + done : low + until, step * 128 : (step + 1) * 128]
        folded[done:until, :] = total
        done = until
    return folded[2 : keep + 2, 0:64] + folded[1 : keep + 1, 64:128]


def soft(moved, bound):
    return jnp.where(moved > 0, 1.0, -1.0) * jnp.maximum(jnp.abs(moved) - bound, 0.0)


def second_kernel(
    left_any, middle, right_any, lags, own_gradient, border, peak, step, valid, *rest
):
    outs, scratch, kept = rest[:-12], rest[-12:-1], rest[-1]
    signal, codes, codes_low, pairs, windows, wide, spread, folded = scratch[:8]
    left, right, sems = scratch[8:]
    near = [
        pltpu.make_async_copy(
            left_any.at[:, pl.ds(left_any.shape[1] - HALO, HALO)], left, sems.at[COARSE]),
        pltpu.make_async_copy(right_any.at[:, pl.ds(0, HALO)], right, sems.at[COARSE + 1]),
    ]
    for copy in near:
        copy.start()
    for copy in near:
        copy.wait()
    width = middle.shape[1]
    step_size = step[0]
    threshold = SPARSITY * jnp.max(peak[...])
    bound = step_size * threshold
    low, high = valid[0], valid[1]
    whole = jnp.concatenate([left[...], middle[...], right[...]], 1)
    signal[...] = whole.T

    def row(start, count):
        return lax.broadcasted_iota(jnp.int32, (count, 1), 0) + start

    for start, values in (
        (0, border[0:HALO, :]),
        (HALO, own_gradient[...]),
        (HALO + width, border[HALO:, :]),
    ):
        count = values.shape[0]
        moved = -step_size * (values * SCALE)
        updated = soft(moved, bound)
        if start == 0:
            updated = jnp.where(row(0, count) >= low, updated, 0.0)
        codes[start : start + count, :] = updated
        codes_low[start : start + count, :] = updated.astype(BF16)
    rows2 = width + 2 * ATOM_LEN
    model = forward(codes_low, lags, wide, spread, folded, ATOM_LEN - FINE, rows2 + FINE)
    resid = model * SCALE - signal[ATOM_LEN : ATOM_LEN + rows2, :]
    resid = jnp.where(row(ATOM_LEN, rows2) < high, resid, 0.0)
    pairs[0:rows2, 0:64] = resid
    pairs[0 : rows2 - 1, 64:128] = pairs[1:rows2, 0:64]
    fill_windows(pairs, windows, rows2 - FINE)
    rows3 = width + ATOM_LEN
    for begin, end in row_chunks(rows3):
        target = spread.at[pl.ds(begin, end - begin), 0:ATOMS]
        adjoint(windows, lags, target, [(begin, end - begin)])
    before = codes[ATOM_LEN : ATOM_LEN + rows3, :]
    moved = before - step_size * (spread[0:rows3, 0:ATOMS] * SCALE)
    updated = jnp.where(row(ATOM_LEN, rows3) >= low, soft(moved, bound), 0.0)
    codes[0:rows3, :] = updated
    codes_low[0:rows3, :] = updated.astype(BF16)
    turned = updated.T
    outs[0][...] = turned[:, ATOM_LEN:]
    sparse = jnp.sum(jnp.abs(codes[ATOM_LEN:rows3, :]))
    model = forward(codes_low, lags, wide, spread, folded, ATOM_LEN - FINE, width + FINE)
    resid = model * SCALE - signal[HALO : HALO + width, :]
    resid_low = resid.T.astype(BF16)
    ahead = turned.astype(BF16)
    loss = 0.5 * jnp.sum(resid * resid) + threshold * sparse
    if len(outs) == 1 + PEERS:
        atoms = ATOMS // PEERS
        whole_loss = jnp.full((16, ATOM_LEN), loss, F32)
        high_part = whole_loss.astype(BF16)
        rest_loss = whole_loss - high_part.astype(F32)
        middle_part = rest_loss.astype(BF16)
        low_part = (rest_loss - middle_part.astype(F32)).astype(BF16)
        lane = lax.broadcasted_iota(jnp.int32, (16, ATOM_LEN), 1)
        tail = jnp.where(
            lane == 0,
            high_part.astype(F32),
            jnp.where(lane == 1, middle_part.astype(F32), low_part.astype(F32)),
        ).astype(BF16)
        kept[...] = ahead
        for turn in range(PEERS):
            first = pl.multiple_of(valid[2 + turn] * atoms, atoms)
            piece = outs[1 + turn]
            piece[0:atoms, :] = kept[pl.ds(first, atoms), ATOM_LEN:]
            piece[atoms : atoms + CHANNELS, :] = resid_low
            for part in range(atoms // 16):
                piece[atoms + CHANNELS :, part * ATOM_LEN : (part + 1) * ATOM_LEN] = kept[
                    pl.ds(pl.multiple_of(first + part * 16, 16), 16), 0:ATOM_LEN
                ]
            piece[atoms + CHANNELS :, HALO : HALO + ATOM_LEN] = tail
            piece[atoms + CHANNELS :, HALO + ATOM_LEN :] = jnp.zeros(
                (16, width - HALO - ATOM_LEN), BF16
            )
    else:
        outs[1][...] = ahead
        outs[2][...] = resid_low
        outs[3][...] = jnp.full((8, 128), loss, F32)


def correlate(codes_of, resid_of, blocks, atoms, width, stack, pairs, windows):
    main = blocks * width
    length = width + ATOM_LEN
    lane = lax.broadcasted_iota(jnp.int32, (atoms, ATOM_LEN), 1)
    extra = [jnp.zeros((atoms, ATOM_LEN), F32) for _ in range(COARSE)]
    windows[main : main + ATOM_LEN, :] = jnp.zeros((ATOM_LEN, WIDE), BF16)
    for block in range(blocks):
        piece = jnp.concatenate(
            [resid_of(block).astype(F32), jnp.zeros((CHANNELS, ATOM_LEN), F32)], 1
        )
        piece = pltpu.roll(piece, FINE, 1)
        both = jnp.concatenate([piece, pltpu.roll(piece, length - 1, 1)], 0)
        slot = pairs.at[block % 2]
        slot[...] = both.T
        for step in range(FINE // 2):
            lanes = slice(step * 128, (step + 1) * 128)
            low = 2 * step
            windows[main + block * FINE : main + (block + 1) * FINE, lanes] = slot[
                low : low + FINE, :
            ].astype(BF16)
            low += FINE
            windows[block * width : (block + 1) * width, lanes] = slot[
                low : low + width, :
            ].astype(BF16)
        held = codes_of(block).astype(F32)
        for coarse in range(COARSE):
            start = ATOM_LEN - coarse * FINE
            turned = pltpu.roll(held, length - start, 1)
            stack[coarse * atoms : (coarse + 1) * atoms, block * width : (block + 1) * width] = (
                turned[:, :width].astype(BF16)
            )
            turned = pltpu.roll(held, (FINE * block - (start - FINE)) % length, 1)[:, :ATOM_LEN]
            inside = (lane >= FINE * block) & (lane < FINE * (block + 1))
            extra[coarse] = jnp.where(inside, turned, extra[coarse])
    for coarse in range(COARSE):
        stack[coarse * atoms : (coarse + 1) * atoms, main : main + ATOM_LEN] = extra[coarse].astype(
            BF16
        )
    half = WIDE // 2
    return jnp.concatenate(
        [
            jnp.dot(stack[...], windows[:, low : low + half], preferred_element_type=F32)
            for low in (0, half)
        ],
        1,
    )


def shared_part(pieces, stack, pairs, windows):
    rows, width = pieces[0].shape
    atoms = rows - CHANNELS - 16

    def codes_of(block):
        before = [
            pieces[block][atoms + CHANNELS :, part * ATOM_LEN : (part + 1) * ATOM_LEN]
            for part in range(atoms // 16)
        ]
        return jnp.concatenate(
            [jnp.concatenate(before, 0).astype(F32), pieces[block][0:atoms, :].astype(F32)], 1
        )

    def resid_of(block):
        return pieces[block][atoms : atoms + CHANNELS, :]

    loss = jnp.zeros((16, ATOM_LEN), F32)
    for piece in pieces:
        loss += piece[atoms + CHANNELS :, HALO : HALO + ATOM_LEN].astype(F32)
    lane = lax.broadcasted_iota(jnp.int32, (16, ATOM_LEN), 1)
    loss = jnp.sum(jnp.where(lane < 3, loss, 0.0), 1, keepdims=True)[0:8]
    total = correlate(
        codes_of, resid_of, len(pieces), atoms, width, stack, pairs, windows
    )
    return total, jnp.broadcast_to(loss, (8, WIDE))


def shared_first(*refs):
    pieces, (out, stack, pairs, windows) = refs[: PEERS // 2], refs[PEERS // 2 :]
    total, loss = shared_part(pieces, stack, pairs, windows)
    rows = total.shape[0]
    out[0:rows, :] = total
    out[rows:, :] = loss


def shared_second(core, before, *refs):
    pieces, (keep, give, stack, pairs, windows, total) = refs[: PEERS // 2], refs[PEERS // 2 :]
    sums, loss = shared_part(pieces, stack, pairs, windows)
    rows = total.shape[0]
    atoms = rows // COARSE
    total[...] = sums + before[0:rows, :]
    half = atoms // 2
    mine = core[0] * half
    other = half - mine
    for coarse in range(COARSE):
        rows_of = slice(coarse * half, (coarse + 1) * half)
        keep[rows_of, :] = total[pl.ds(coarse * atoms + mine, half), :]
        give[rows_of, :] = total[pl.ds(coarse * atoms + other, half), :]
    ending = loss + before[rows:, :]
    keep[COARSE * half :, :] = ending
    give[COARSE * half :, :] = ending


def lone_kernel(codes, resid, out, stack, pairs, windows):
    out[...] = correlate(
        lambda b: codes[...], lambda b: resid[...], 1, ATOMS, resid.shape[1], stack, pairs, windows
    )


def last_kernel(inverse, keep, recv_any, atoms_ref, out, loss_out, total, turned, recv, sem):
    copy = pltpu.make_async_copy(recv_any, recv, sem.at[0])
    copy.start()
    copy.wait()
    half = atoms_ref.shape[0]
    loss_out[0] = (keep[COARSE * half, 0] + recv[COARSE * half, 0]) * inverse
    for step in range(FINE // 2):
        lanes = slice(step * 128, (step + 1) * 128)
        total[step] = keep[0 : COARSE * half, lanes] + recv[0 : COARSE * half, lanes]
    for pair in range(half // 2):
        for step in range(FINE // 2):
            one = total.at[step][pl.ds(2 * pair, COARSE, stride=half), :]
            two = total.at[step][pl.ds(2 * pair + 1, COARSE, stride=half), :]
            block = turned.at[pair]
            block[pl.ds(2 * step, COARSE, stride=FINE), :] = jnp.concatenate(
                [one[:, 0:64], two[:, 0:64]], 1
            )
            block[pl.ds(2 * step + 1, COARSE, stride=FINE), :] = jnp.concatenate(
                [one[:, 64:128], two[:, 64:128]], 1
            )
    gradient = jnp.concatenate([turned[pair].T for pair in range(half // 2)], 0)
    gradient = gradient.reshape(half, CHANNELS, ATOM_LEN)
    normed = gradient / jnp.sqrt(
        jnp.mean(gradient * gradient, axis=(1, 2), keepdims=True) + EPSILON
    )
    moved = atoms_ref[...].astype(F32) - DICT_RATE * normed
    out[...] = moved / jnp.sqrt(jnp.mean(moved * moved, axis=(1, 2), keepdims=True) + EPSILON)


def body(signal, dictionary, step):
    width = signal.shape[1]
    count = lax.axis_size("tm")
    me = lax.axis_index("tm")
    left = shifted(signal, "tm", 1)
    right = shifted(signal, "tm", -1)
    rows1 = width + 3 * ATOM_LEN
    span = width + 2 * HALO

    near_scratch = [pltpu.VMEM((CHANNELS, HALO), F32)]
    sems = [pltpu.SemaphoreType.DMA((COARSE + 2,))]
    bordered = width + ATOM_LEN
    gradient, peak, lags = pl.pallas_call(
        own_kernel,
        out_shape=(
            jax.ShapeDtypeStruct((width, ATOMS), F32),
            jax.ShapeDtypeStruct((count, 8, 128), F32),
            jax.ShapeDtypeStruct((ATOM_LEN * CHANNELS, ATOMS), BF16),
        ),
        in_specs=[vmem(), anywhere(), pl.BlockSpec(memory_space=pltpu.HBM)],
        out_specs=(vmem(), vmem(), pl.BlockSpec(memory_space=pltpu.HBM)),
        scratch_shapes=near_scratch
        + [pltpu.VMEM(dictionary.shape, BF16)]
        + [pltpu.VMEM((ATOM_LEN * CHANNELS, ATOMS), BF16)]
        + [pltpu.VMEM((ATOM_LEN * PITCH, 128), F32)] * 2
        + [pltpu.VMEM((bordered, 128), F32), pltpu.VMEM((bordered, WIDE), BF16)]
        + sems
        + [pltpu.SemaphoreType.DMA((2,))],
        compiler_params=kernel_params(OWN_LIMIT),
        cost_estimate=cost(2 * width * ATOMS * WIDE * COARSE, 5 << 20),
    )(signal, right, dictionary)
    peak = lax.all_to_all(peak, "tm", 0, 0, tiled=False)
    span_border = 2 * HALO + ATOM_LEN
    border = pl.pallas_call(
        border_kernel,
        out_shape=jax.ShapeDtypeStruct((HALO + ATOM_LEN, ATOMS), F32),
        in_specs=[anywhere(), vmem(), anywhere(), vmem()],
        out_specs=vmem(),
        scratch_shapes=near_scratch * 2
        + [pltpu.VMEM((span_border, 128), F32), pltpu.VMEM((span_border, WIDE), BF16)]
        + sems,
        compiler_params=kernel_params(),
        cost_estimate=cost(2 * (HALO + ATOM_LEN) * ATOMS * WIDE * COARSE, 5 << 20),
    )(left, signal, right, lags)

    valid = jnp.stack(
        [jnp.where(me == 0, HALO, 0), jnp.where(me == count - 1, HALO + width, span)]
        + [(me // 2) ^ turn for turn in range(PEERS)]
    ).astype(jnp.int32)
    owned = ATOMS // count
    shared = count == 2 * PEERS
    own_atoms = lax.dynamic_slice_in_dim(dictionary, me * owned, owned, 0)
    if shared:
        rows = ATOMS // PEERS + CHANNELS + 16
        outs = (jax.ShapeDtypeStruct((rows, width), BF16),) * PEERS
    else:
        outs = (
            jax.ShapeDtypeStruct((ATOMS, width + ATOM_LEN), BF16),
            jax.ShapeDtypeStruct((CHANNELS, width), BF16),
            jax.ShapeDtypeStruct((8, 128), F32),
        )
    codes, *others = pl.pallas_call(
        second_kernel,
        out_shape=(jax.ShapeDtypeStruct((ATOMS, width), F32),) + outs,
        in_specs=[anywhere(), vmem(), anywhere(), vmem()] + [vmem()] * 3 + [smem()] * 2,
        out_specs=(vmem(),) * (1 + len(outs)),
        scratch_shapes=[
            pltpu.VMEM((span, CHANNELS), F32),
            pltpu.VMEM((rows1, ATOMS), F32),
            pltpu.VMEM((rows1, ATOMS), BF16),
            pltpu.VMEM((rows1, 128), F32),
            pltpu.VMEM((rows1, WIDE), BF16),
            pltpu.VMEM((rows1, COARSE * ATOMS), BF16),
            pltpu.VMEM((rows1, WIDE), F32),
            pltpu.VMEM((rows1, 128), F32),
        ]
        + near_scratch * 2
        + sems
        + [pltpu.VMEM((ATOMS, width + ATOM_LEN), BF16)],
        compiler_params=kernel_params(),
    )(left, signal, right, lags, gradient, border, peak, step, valid)

    def correlate_scratch(blocks, atoms):
        return [
            pltpu.VMEM((COARSE * atoms, blocks * width + ATOM_LEN), BF16),
            pltpu.VMEM((2, width + ATOM_LEN, 128), F32),
            pltpu.VMEM((blocks * width + ATOM_LEN, WIDE), BF16),
        ]

    inverse = 1.0 / (CHANNELS * width * count)
    if shared:
        core = me % 2
        pieces = list(others)
        for turn in range(1, PEERS):
            pieces[turn] = swapped(pieces[turn], 2 * turn)
        half_rows = jax.ShapeDtypeStruct((COARSE * owned + 8, WIDE), F32)
        blocks = PEERS // 2
        before = pl.pallas_call(
            shared_first,
            out_shape=jax.ShapeDtypeStruct((COARSE * 2 * owned + 8, WIDE), F32),
            in_specs=[vmem()] * blocks,
            out_specs=vmem(),
            scratch_shapes=correlate_scratch(blocks, 2 * owned),
            compiler_params=kernel_params(),
            cost_estimate=cost(2 * COARSE * 2 * owned * blocks * width * WIDE, 2 << 20),
        )(*[pieces[turn] for turn in (0, 4, 5, 6)])
        keep, give = pl.pallas_call(
            shared_second,
            out_shape=(half_rows, half_rows),
            in_specs=[smem(), vmem()] + [vmem()] * blocks,
            out_specs=(vmem(), vmem()),
            scratch_shapes=correlate_scratch(blocks, 2 * owned)
            + [pltpu.VMEM((COARSE * 2 * owned, WIDE), F32)],
            compiler_params=kernel_params(),
            cost_estimate=cost(2 * COARSE * 2 * owned * blocks * width * WIDE, 2 << 20),
        )(core.reshape(1).astype(jnp.int32), before, *[pieces[turn] for turn in (7, 3, 2, 1)])
        recv = swapped(give, 1)
        new_dictionary, loss = pl.pallas_call(
            lambda *refs: last_kernel(inverse, *refs),
            out_shape=(
                jax.ShapeDtypeStruct((owned, CHANNELS, ATOM_LEN), F32),
                jax.ShapeDtypeStruct((1,), F32),
            ),
            in_specs=[vmem(), anywhere(), vmem()],
            out_specs=(vmem(), smem()),
            scratch_shapes=[
                pltpu.VMEM((FINE // 2, COARSE * owned, 128), F32),
                pltpu.VMEM((owned // 2, ATOM_LEN, 2 * CHANNELS), F32),
                pltpu.VMEM(half_rows.shape, F32),
                pltpu.SemaphoreType.DMA((1,)),
            ],
            compiler_params=kernel_params(),
        )(keep, recv, own_atoms)
        return (codes, new_dictionary, loss)

    ahead, resid, loss = others
    part = pl.pallas_call(
        lone_kernel,
        out_shape=jax.ShapeDtypeStruct((COARSE * ATOMS, WIDE), F32),
        in_specs=[vmem()] * 2,
        out_specs=vmem(),
        scratch_shapes=correlate_scratch(1, ATOMS),
        compiler_params=kernel_params(),
    )(ahead, resid)
    summed = lax.psum_scatter(
        part.reshape(COARSE, ATOMS, WIDE), "tm", scatter_dimension=1, tiled=True
    )
    atom_gradient = (
        summed.reshape(COARSE, owned, FINE, CHANNELS)
        .transpose(1, 3, 0, 2)
        .reshape(owned, CHANNELS, ATOM_LEN)
    )
    normed = atom_gradient / jnp.sqrt(
        jnp.mean(atom_gradient * atom_gradient, axis=(1, 2), keepdims=True) + EPSILON
    )
    moved = own_atoms.astype(F32) - DICT_RATE * normed
    new_dictionary = moved / jnp.sqrt(
        jnp.mean(moved * moved, axis=(1, 2), keepdims=True) + EPSILON
    )
    bit = 1
    while bit < count:
        loss = loss + swapped(loss, bit)
        bit *= 2
    return (codes, new_dictionary, loss[0, :1] * inverse)


def solution(mesh):
    return jax.shard_map(
        body,
        mesh=mesh,
        in_specs=(P(None, ("groups", "tm")), P(), P()),
        out_specs=(P(None, ("groups", "tm")), P(("groups", "tm"), None, None), P("groups")),
        check_vma=False,
    )
```

```python
import math

import jax
import jax.numpy as jnp
from jax import lax
from jax.experimental import pallas as pl
from jax.experimental.pallas import tpu as pltpu
from jax.sharding import PartitionSpec as P

ATOMS = 256
CHANNELS = 64
ATOM_LEN = 128
SPARSITY = 0.05
DICT_RATE = 0.5
EPSILON = 1e-06

SCALE = 1.0 / math.sqrt(CHANNELS * ATOM_LEN)
FINE = 16
COARSE = ATOM_LEN // FINE
WIDE = FINE * CHANNELS
HALO = 2 * ATOM_LEN
F32 = jnp.float32
BF16 = jnp.bfloat16
PITCH = CHANNELS + 8
CHUNKS = 2
PEERS = 8
OWN_LIMIT = 53 * 1024 * 1024
VMEM_LIMIT = 36 * 1024 * 1024


def vmem():
    return pl.BlockSpec(memory_space=pltpu.VMEM)


def smem():
    return pl.BlockSpec(memory_space=pltpu.SMEM)


def anywhere():
    return pl.BlockSpec(memory_space=pl.ANY)


def fetch_lags(source, lags, arrived):
    copies = [
        pltpu.make_async_copy(
            source.at[pl.ds(coarse * WIDE, WIDE), :],
            lags.at[pl.ds(coarse * WIDE, WIDE), :],
            arrived.at[coarse],
        )
        for coarse in range(COARSE)
    ]
    for copy in copies:
        copy.start()
    return copies


def cost(flops, bytes_accessed):
    return pl.CostEstimate(flops=flops, bytes_accessed=bytes_accessed, transcendentals=0)


def kernel_params(limit=VMEM_LIMIT):
    return pltpu.CompilerParams(vmem_limit_bytes=limit)


def shifted(value, axis, steps):
    count = lax.axis_size(axis)
    leading, last = (max(0, -steps), min(count, count - steps))
    return lax.ppermute(value, axis, [(source, source + steps) for source in range(leading, last)])


def swapped(value, bit):
    count = lax.axis_size("tm")
    return lax.ppermute(value, "tm", [(i, i ^ bit) for i in range(count)])


def fill_windows(pairs, windows, rows):
    for step in range(FINE // 2):
        windows[0:rows, step * 128 : (step + 1) * 128] = pairs[
            2 * step : 2 * step + rows, :
        ].astype(BF16)


def adjoint(windows, lags, total, spans, copies=None):
    rows = sum(count for _, count in spans)
    for coarse in range(COARSE):
        if copies is not None:
            copies[coarse].wait()
        shift = coarse * FINE
        taken = [windows[start + shift : start + shift + count, :] for start, count in spans]
        part = jnp.dot(
            taken[0] if len(taken) == 1 else jnp.concatenate(taken, 0),
            lags[coarse * WIDE : (coarse + 1) * WIDE, :],
            preferred_element_type=F32,
        )
        if coarse == 0:
            total[0:rows, :] = part
        else:
            total[0:rows, :] += part


def windows_of(whole, pairs, windows):
    length = whole.shape[1]
    both = jnp.concatenate([whole, pltpu.roll(whole, length - 1, 1)], 0)
    pairs[0:length, :] = both.T
    fill_windows(pairs, windows, length - FINE)


def turn_dictionary(atoms, lags, by_atom, by_lag, copies):
    half = ATOMS // 2
    for part in range(2):
        copies[part].wait()
        for atom in range(half):
            by_atom[atom * PITCH : atom * PITCH + CHANNELS, :] = atoms[part * half + atom].astype(
                F32
            )
        for channel in range(CHANNELS):
            turned = by_atom[pl.ds(channel, half, stride=PITCH), :].T
            by_lag[pl.ds(channel, ATOM_LEN, stride=PITCH), :] = turned
        for lag in range(ATOM_LEN):
            lags[lag * CHANNELS : (lag + 1) * CHANNELS, part * half : (part + 1) * half] = by_lag[
                lag * PITCH : lag * PITCH + CHANNELS, :
            ].astype(BF16)


def own_kernel(
    middle, right_any, atoms_any, gradient, largest, lags_out,
    right, atoms, lags, by_atom, by_lag, pairs, windows, sems, atom_sems,
):
    width = middle.shape[1]
    half = ATOMS // 2
    loads = [
        pltpu.make_async_copy(
            atoms_any.at[pl.ds(part * half, half)],
            atoms.at[pl.ds(part * half, half)],
            atom_sems.at[part],
        )
        for part in range(2)
    ]
    loads[0].start()
    near = pltpu.make_async_copy(right_any.at[:, pl.ds(0, HALO)], right, sems.at[COARSE])
    near.start()
    loads[1].start()
    near.wait()
    whole = jnp.concatenate([middle[...], right[:, 0:ATOM_LEN]], 1)
    windows_of(-whole, pairs, windows)
    turn_dictionary(atoms, lags, by_atom, by_lag, loads)
    copies = fetch_lags(lags, lags_out, sems)
    for begin, end in row_chunks(width):
        adjoint(windows, lags, gradient.at[pl.ds(begin, end - begin), :], [(begin, end - begin)])
    own = jnp.abs(gradient[...]) * SCALE
    folded = jnp.max(own.reshape(width // 8, 8, ATOMS), 0)
    folded = jnp.maximum(folded[:, :128], folded[:, 128:])
    for peer in range(largest.shape[0]):
        largest[peer] = folded
    for copy in copies:
        copy.wait()


def border_kernel(
    left_any, middle, right_any, lags, gradient, left, right, pairs, windows, sems
):
    near = [
        pltpu.make_async_copy(
            left_any.at[:, pl.ds(left_any.shape[1] - HALO, HALO)], left, sems.at[COARSE]),
        pltpu.make_async_copy(right_any.at[:, pl.ds(0, HALO)], right, sems.at[COARSE + 1]),
    ]
    for copy in near:
        copy.start()
    for copy in near:
        copy.wait()
    whole = jnp.concatenate([left[...], middle[:, 0:ATOM_LEN], right[...]], 1)
    windows_of(-whole, pairs, windows)
    adjoint(windows, lags, gradient.at[pl.ds(0, HALO), :], [(0, HALO)])
    adjoint(windows, lags, gradient.at[pl.ds(HALO, ATOM_LEN), :], [(HALO + ATOM_LEN, ATOM_LEN)])


def row_chunks(rows):
    size = -(-rows // (CHUNKS * FINE)) * FINE
    return [(low, min(low + size, rows)) for low in range(0, rows, size)]


def forward(codes, lags, wide, spread, folded, start, rows):
    keep = rows - FINE
    weights = jnp.concatenate(
        [lags[coarse * WIDE : (coarse + 1) * WIDE, :] for coarse in range(COARSE)], 1
    )
    done = 0
    for begin, end in row_chunks(rows):
        for coarse in range(COARSE):
            low = start + begin - coarse * FINE
            wide[begin:end, coarse * ATOMS : (coarse + 1) * ATOMS] = codes[
                low : low + end - begin, :
            ]
        spread[begin:end, :] = lax.dot_general(
            wide[begin:end, :], weights, (((1,), (1,)), ((), ())), preferred_element_type=F32
        )
        until = keep + 2 if end == rows else end - FINE
        total = spread[FINE - 2 + done : FINE - 2 + until, 0:128]
        for step in range(1, FINE // 2):
            low = FINE - 2 - 2 * step
            total = total + spread[low + done : low + until, step * 128 : (step + 1) * 128]
        folded[done:until, :] = total
        done = until
    return folded[2 : keep + 2, 0:64] + folded[1 : keep + 1, 64:128]


def soft(moved, bound):
    return jnp.where(moved > 0, 1.0, -1.0) * jnp.maximum(jnp.abs(moved) - bound, 0.0)


def second_kernel(
    left_any, middle, right_any, lags, own_gradient, border, peak, step, valid, *rest
):
    outs, scratch, kept = rest[:-12], rest[-12:-1], rest[-1]
    signal, codes, codes_low, pairs, windows, wide, spread, folded = scratch[:8]
    left, right, sems = scratch[8:]
    near = [
        pltpu.make_async_copy(
            left_any.at[:, pl.ds(left_any.shape[1] - HALO, HALO)], left, sems.at[COARSE]),
        pltpu.make_async_copy(right_any.at[:, pl.ds(0, HALO)], right, sems.at[COARSE + 1]),
    ]
    for copy in near:
        copy.start()
    for copy in near:
        copy.wait()
    width = middle.shape[1]
    step_size = step[0]
    threshold = SPARSITY * jnp.max(peak[...])
    bound = step_size * threshold
    low, high = valid[0], valid[1]
    whole = jnp.concatenate([left[...], middle[...], right[...]], 1)
    signal[...] = whole.T

    def row(start, count):
        return lax.broadcasted_iota(jnp.int32, (count, 1), 0) + start

    for start, values in (
        (0, border[0:HALO, :]),
        (HALO, own_gradient[...]),
        (HALO + width, border[HALO:, :]),
    ):
        count = values.shape[0]
        moved = -step_size * (values * SCALE)
        updated = soft(moved, bound)
        if start == 0:
            updated = jnp.where(row(0, count) >= low, updated, 0.0)
        codes[start : start + count, :] = updated
        codes_low[start : start + count, :] = updated.astype(BF16)
    rows2 = width + 2 * ATOM_LEN
    model = forward(codes_low, lags, wide, spread, folded, ATOM_LEN - FINE, rows2 + FINE)
    resid = model * SCALE - signal[ATOM_LEN : ATOM_LEN + rows2, :]
    resid = jnp.where(row(ATOM_LEN, rows2) < high, resid, 0.0)
    pairs[0:rows2, 0:64] = resid
    pairs[0 : rows2 - 1, 64:128] = pairs[1:rows2, 0:64]
    fill_windows(pairs, windows, rows2 - FINE)
    rows3 = width + ATOM_LEN
    for begin, end in row_chunks(rows3):
        target = spread.at[pl.ds(begin, end - begin), 0:ATOMS]
        adjoint(windows, lags, target, [(begin, end - begin)])
    before = codes[ATOM_LEN : ATOM_LEN + rows3, :]
    moved = before - step_size * (spread[0:rows3, 0:ATOMS] * SCALE)
    updated = jnp.where(row(ATOM_LEN, rows3) >= low, soft(moved, bound), 0.0)
    codes[0:rows3, :] = updated
    codes_low[0:rows3, :] = updated.astype(BF16)
    turned = updated.T
    outs[0][...] = turned[:, ATOM_LEN:]
    sparse = jnp.sum(jnp.abs(codes[ATOM_LEN:rows3, :]))
    model = forward(codes_low, lags, wide, spread, folded, ATOM_LEN - FINE, width + FINE)
    resid = model * SCALE - signal[HALO : HALO + width, :]
    resid_low = resid.T.astype(BF16)
    ahead = turned.astype(BF16)
    loss = 0.5 * jnp.sum(resid * resid) + threshold * sparse
    if len(outs) == 1 + PEERS:
        atoms = ATOMS // PEERS
        whole_loss = jnp.full((16, ATOM_LEN), loss, F32)
        high_part = whole_loss.astype(BF16)
        rest_loss = whole_loss - high_part.astype(F32)
        middle_part = rest_loss.astype(BF16)
        low_part = (rest_loss - middle_part.astype(F32)).astype(BF16)
        lane = lax.broadcasted_iota(jnp.int32, (16, ATOM_LEN), 1)
        tail = jnp.where(
            lane == 0,
            high_part.astype(F32),
            jnp.where(lane == 1, middle_part.astype(F32), low_part.astype(F32)),
        ).astype(BF16)
        kept[...] = ahead
        for turn in range(PEERS):
            first = pl.multiple_of(valid[2 + turn] * atoms, atoms)
            piece = outs[1 + turn]
            piece[0:atoms, :] = kept[pl.ds(first, atoms), ATOM_LEN:]
            piece[atoms : atoms + CHANNELS, :] = resid_low
            for part in range(atoms // 16):
                piece[atoms + CHANNELS :, part * ATOM_LEN : (part + 1) * ATOM_LEN] = kept[
                    pl.ds(pl.multiple_of(first + part * 16, 16), 16), 0:ATOM_LEN
                ]
            piece[atoms + CHANNELS :, HALO : HALO + ATOM_LEN] = tail
            piece[atoms + CHANNELS :, HALO + ATOM_LEN :] = jnp.zeros(
                (16, width - HALO - ATOM_LEN), BF16
            )
    else:
        outs[1][...] = ahead
        outs[2][...] = resid_low
        outs[3][...] = jnp.full((8, 128), loss, F32)


def correlate(codes_of, resid_of, blocks, atoms, width, stack, pairs, windows):
    main = blocks * width
    length = width + ATOM_LEN
    lane = lax.broadcasted_iota(jnp.int32, (atoms, ATOM_LEN), 1)
    extra = [jnp.zeros((atoms, ATOM_LEN), F32) for _ in range(COARSE)]
    windows[main : main + ATOM_LEN, :] = jnp.zeros((ATOM_LEN, WIDE), BF16)
    sums = None
    for block in range(blocks):
        piece = jnp.concatenate(
            [resid_of(block).astype(F32), jnp.zeros((CHANNELS, ATOM_LEN), F32)], 1
        )
        piece = pltpu.roll(piece, FINE, 1)
        both = jnp.concatenate([piece, pltpu.roll(piece, length - 1, 1)], 0)
        slot = pairs.at[block % 2]
        slot[...] = both.T
        for step in range(FINE // 2):
            lanes = slice(step * 128, (step + 1) * 128)
            low = 2 * step
            windows[main + block * FINE : main + (block + 1) * FINE, lanes] = slot[
                low : low + FINE, :
            ].astype(BF16)
            low += FINE
            windows[block * width : (block + 1) * width, lanes] = slot[
                low : low + width, :
            ].astype(BF16)
        held = codes_of(block).astype(F32)
        for coarse in range(COARSE):
            start = ATOM_LEN - coarse * FINE
            turned = pltpu.roll(held, length - start, 1)
            stack[coarse * atoms : (coarse + 1) * atoms, block * width : (block + 1) * width] = (
                turned[:, :width].astype(BF16)
            )
            turned = pltpu.roll(held, (FINE * block - (start - FINE)) % length, 1)[:, :ATOM_LEN]
            inside = (lane >= FINE * block) & (lane < FINE * (block + 1))
            extra[coarse] = jnp.where(inside, turned, extra[coarse])
        if block % 2 == 1 or block == blocks - 1:
            begin = block // 2 * 2 * width
            end = (block + 1) * width
            part = jnp.dot(
                stack[:, begin:end], windows[begin:end, :], preferred_element_type=F32
            )
            sums = part if sums is None else sums + part
    for coarse in range(COARSE):
        stack[coarse * atoms : (coarse + 1) * atoms, main : main + ATOM_LEN] = extra[coarse].astype(
            BF16
        )
    return sums + jnp.dot(
        stack[:, main : main + ATOM_LEN],
        windows[main : main + ATOM_LEN, :],
        preferred_element_type=F32,
    )


def shared_part(pieces, stack, pairs, windows):
    rows, width = pieces[0].shape
    atoms = rows - CHANNELS - 16

    def codes_of(block):
        before = [
            pieces[block][atoms + CHANNELS :, part * ATOM_LEN : (part + 1) * ATOM_LEN]
            for part in range(atoms // 16)
        ]
        return jnp.concatenate(
            [jnp.concatenate(before, 0).astype(F32), pieces[block][0:atoms, :].astype(F32)], 1
        )

    def resid_of(block):
        return pieces[block][atoms : atoms + CHANNELS, :]

    loss = jnp.zeros((16, ATOM_LEN), F32)
    for piece in pieces:
        loss += piece[atoms + CHANNELS :, HALO : HALO + ATOM_LEN].astype(F32)
    lane = lax.broadcasted_iota(jnp.int32, (16, ATOM_LEN), 1)
    loss = jnp.sum(jnp.where(lane < 3, loss, 0.0), 1, keepdims=True)[0:8]
    total = correlate(
        codes_of, resid_of, len(pieces), atoms, width, stack, pairs, windows
    )
    return total, jnp.broadcast_to(loss, (8, WIDE))


def shared_first(*refs):
    pieces, (out, stack, pairs, windows) = refs[: PEERS // 2], refs[PEERS // 2 :]
    total, loss = shared_part(pieces, stack, pairs, windows)
    rows = total.shape[0]
    out[0:rows, :] = total
    out[rows:, :] = loss


def shared_second(core, before, *refs):
    pieces, (keep, give, stack, pairs, windows, total) = refs[: PEERS // 2], refs[PEERS // 2 :]
    sums, loss = shared_part(pieces, stack, pairs, windows)
    rows = total.shape[0]
    atoms = rows // COARSE
    total[...] = sums + before[0:rows, :]
    half = atoms // 2
    mine = core[0] * half
    other = half - mine
    for coarse in range(COARSE):
        rows_of = slice(coarse * half, (coarse + 1) * half)
        keep[rows_of, :] = total[pl.ds(coarse * atoms + mine, half), :]
        give[rows_of, :] = total[pl.ds(coarse * atoms + other, half), :]
    ending = loss + before[rows:, :]
    keep[COARSE * half :, :] = ending
    give[COARSE * half :, :] = ending


def lone_kernel(codes, resid, out, stack, pairs, windows):
    out[...] = correlate(
        lambda b: codes[...], lambda b: resid[...], 1, ATOMS, resid.shape[1], stack, pairs, windows
    )


def last_kernel(inverse, keep, recv_any, atoms_ref, out, loss_out, total, turned, recv, sem):
    copy = pltpu.make_async_copy(recv_any, recv, sem.at[0])
    copy.start()
    copy.wait()
    half = atoms_ref.shape[0]
    loss_out[0] = (keep[COARSE * half, 0] + recv[COARSE * half, 0]) * inverse
    for step in range(FINE // 2):
        lanes = slice(step * 128, (step + 1) * 128)
        total[step] = keep[0 : COARSE * half, lanes] + recv[0 : COARSE * half, lanes]
    for pair in range(half // 2):
        for step in range(FINE // 2):
            one = total.at[step][pl.ds(2 * pair, COARSE, stride=half), :]
            two = total.at[step][pl.ds(2 * pair + 1, COARSE, stride=half), :]
            block = turned.at[pair]
            block[pl.ds(2 * step, COARSE, stride=FINE), :] = jnp.concatenate(
                [one[:, 0:64], two[:, 0:64]], 1
            )
            block[pl.ds(2 * step + 1, COARSE, stride=FINE), :] = jnp.concatenate(
                [one[:, 64:128], two[:, 64:128]], 1
            )
    gradient = jnp.concatenate([turned[pair].T for pair in range(half // 2)], 0)
    gradient = gradient.reshape(half, CHANNELS, ATOM_LEN)
    normed = gradient / jnp.sqrt(
        jnp.mean(gradient * gradient, axis=(1, 2), keepdims=True) + EPSILON
    )
    moved = atoms_ref[...].astype(F32) - DICT_RATE * normed
    out[...] = moved / jnp.sqrt(jnp.mean(moved * moved, axis=(1, 2), keepdims=True) + EPSILON)


def body(signal, dictionary, step):
    width = signal.shape[1]
    count = lax.axis_size("tm")
    me = lax.axis_index("tm")
    left = shifted(signal, "tm", 1)
    right = shifted(signal, "tm", -1)
    rows1 = width + 3 * ATOM_LEN
    span = width + 2 * HALO

    near_scratch = [pltpu.VMEM((CHANNELS, HALO), F32)]
    sems = [pltpu.SemaphoreType.DMA((COARSE + 2,))]
    bordered = width + ATOM_LEN
    gradient, peak, lags = pl.pallas_call(
        own_kernel,
        out_shape=(
            jax.ShapeDtypeStruct((width, ATOMS), F32),
            jax.ShapeDtypeStruct((count, 8, 128), F32),
            jax.ShapeDtypeStruct((ATOM_LEN * CHANNELS, ATOMS), BF16),
        ),
        in_specs=[vmem(), anywhere(), pl.BlockSpec(memory_space=pltpu.HBM)],
        out_specs=(vmem(), vmem(), pl.BlockSpec(memory_space=pltpu.HBM)),
        scratch_shapes=near_scratch
        + [pltpu.VMEM(dictionary.shape, BF16)]
        + [pltpu.VMEM((ATOM_LEN * CHANNELS, ATOMS), BF16)]
        + [pltpu.VMEM((ATOM_LEN * PITCH, 128), F32)] * 2
        + [pltpu.VMEM((bordered, 128), F32), pltpu.VMEM((bordered, WIDE), BF16)]
        + sems
        + [pltpu.SemaphoreType.DMA((2,))],
        compiler_params=kernel_params(OWN_LIMIT),
        cost_estimate=cost(2 * width * ATOMS * WIDE * COARSE, 5 << 20),
    )(signal, right, dictionary)
    peak = lax.all_to_all(peak, "tm", 0, 0, tiled=False)
    span_border = 2 * HALO + ATOM_LEN
    border = pl.pallas_call(
        border_kernel,
        out_shape=jax.ShapeDtypeStruct((HALO + ATOM_LEN, ATOMS), F32),
        in_specs=[anywhere(), vmem(), anywhere(), vmem()],
        out_specs=vmem(),
        scratch_shapes=near_scratch * 2
        + [pltpu.VMEM((span_border, 128), F32), pltpu.VMEM((span_border, WIDE), BF16)]
        + sems,
        compiler_params=kernel_params(),
        cost_estimate=cost(2 * (HALO + ATOM_LEN) * ATOMS * WIDE * COARSE, 5 << 20),
    )(left, signal, right, lags)

    valid = jnp.stack(
        [jnp.where(me == 0, HALO, 0), jnp.where(me == count - 1, HALO + width, span)]
        + [(me // 2) ^ turn for turn in range(PEERS)]
    ).astype(jnp.int32)
    owned = ATOMS // count
    shared = count == 2 * PEERS
    own_atoms = lax.dynamic_slice_in_dim(dictionary, me * owned, owned, 0)
    if shared:
        rows = ATOMS // PEERS + CHANNELS + 16
        outs = (jax.ShapeDtypeStruct((rows, width), BF16),) * PEERS
    else:
        outs = (
            jax.ShapeDtypeStruct((ATOMS, width + ATOM_LEN), BF16),
            jax.ShapeDtypeStruct((CHANNELS, width), BF16),
            jax.ShapeDtypeStruct((8, 128), F32),
        )
    codes, *others = pl.pallas_call(
        second_kernel,
        out_shape=(jax.ShapeDtypeStruct((ATOMS, width), F32),) + outs,
        in_specs=[anywhere(), vmem(), anywhere(), vmem()] + [vmem()] * 3 + [smem()] * 2,
        out_specs=(vmem(),) * (1 + len(outs)),
        scratch_shapes=[
            pltpu.VMEM((span, CHANNELS), F32),
            pltpu.VMEM((rows1, ATOMS), F32),
            pltpu.VMEM((rows1, ATOMS), BF16),
            pltpu.VMEM((rows1, 128), F32),
            pltpu.VMEM((rows1, WIDE), BF16),
            pltpu.VMEM((rows1, COARSE * ATOMS), BF16),
            pltpu.VMEM((rows1, WIDE), F32),
            pltpu.VMEM((rows1, 128), F32),
        ]
        + near_scratch * 2
        + sems
        + [pltpu.VMEM((ATOMS, width + ATOM_LEN), BF16)],
        compiler_params=kernel_params(),
    )(left, signal, right, lags, gradient, border, peak, step, valid)

    def correlate_scratch(blocks, atoms):
        return [
            pltpu.VMEM((COARSE * atoms, blocks * width + ATOM_LEN), BF16),
            pltpu.VMEM((2, width + ATOM_LEN, 128), F32),
            pltpu.VMEM((blocks * width + ATOM_LEN, WIDE), BF16),
        ]

    inverse = 1.0 / (CHANNELS * width * count)
    if shared:
        core = me % 2
        pieces = list(others)
        for turn in range(1, PEERS):
            pieces[turn] = swapped(pieces[turn], 2 * turn)
        half_rows = jax.ShapeDtypeStruct((COARSE * owned + 8, WIDE), F32)
        blocks = PEERS // 2
        before = pl.pallas_call(
            shared_first,
            out_shape=jax.ShapeDtypeStruct((COARSE * 2 * owned + 8, WIDE), F32),
            in_specs=[vmem()] * blocks,
            out_specs=vmem(),
            scratch_shapes=correlate_scratch(blocks, 2 * owned),
            compiler_params=kernel_params(),
            cost_estimate=cost(2 * COARSE * 2 * owned * blocks * width * WIDE, 2 << 20),
        )(*[pieces[turn] for turn in (0, 4, 5, 6)])
        keep, give = pl.pallas_call(
            shared_second,
            out_shape=(half_rows, half_rows),
            in_specs=[smem(), vmem()] + [vmem()] * blocks,
            out_specs=(vmem(), vmem()),
            scratch_shapes=correlate_scratch(blocks, 2 * owned)
            + [pltpu.VMEM((COARSE * 2 * owned, WIDE), F32)],
            compiler_params=kernel_params(),
            cost_estimate=cost(2 * COARSE * 2 * owned * blocks * width * WIDE, 2 << 20),
        )(core.reshape(1).astype(jnp.int32), before, *[pieces[turn] for turn in (7, 3, 2, 1)])
        recv = swapped(give, 1)
        new_dictionary, loss = pl.pallas_call(
            lambda *refs: last_kernel(inverse, *refs),
            out_shape=(
                jax.ShapeDtypeStruct((owned, CHANNELS, ATOM_LEN), F32),
                jax.ShapeDtypeStruct((1,), F32),
            ),
            in_specs=[vmem(), anywhere(), vmem()],
            out_specs=(vmem(), smem()),
            scratch_shapes=[
                pltpu.VMEM((FINE // 2, COARSE * owned, 128), F32),
                pltpu.VMEM((owned // 2, ATOM_LEN, 2 * CHANNELS), F32),
                pltpu.VMEM(half_rows.shape, F32),
                pltpu.SemaphoreType.DMA((1,)),
            ],
            compiler_params=kernel_params(),
        )(keep, recv, own_atoms)
        return (codes, new_dictionary, loss)

    ahead, resid, loss = others
    part = pl.pallas_call(
        lone_kernel,
        out_shape=jax.ShapeDtypeStruct((COARSE * ATOMS, WIDE), F32),
        in_specs=[vmem()] * 2,
        out_specs=vmem(),
        scratch_shapes=correlate_scratch(1, ATOMS),
        compiler_params=kernel_params(),
    )(ahead, resid)
    summed = lax.psum_scatter(
        part.reshape(COARSE, ATOMS, WIDE), "tm", scatter_dimension=1, tiled=True
    )
    atom_gradient = (
        summed.reshape(COARSE, owned, FINE, CHANNELS)
        .transpose(1, 3, 0, 2)
        .reshape(owned, CHANNELS, ATOM_LEN)
    )
    normed = atom_gradient / jnp.sqrt(
        jnp.mean(atom_gradient * atom_gradient, axis=(1, 2), keepdims=True) + EPSILON
    )
    moved = own_atoms.astype(F32) - DICT_RATE * normed
    new_dictionary = moved / jnp.sqrt(
        jnp.mean(moved * moved, axis=(1, 2), keepdims=True) + EPSILON
    )
    bit = 1
    while bit < count:
        loss = loss + swapped(loss, bit)
        bit *= 2
    return (codes, new_dictionary, loss[0, :1] * inverse)


def solution(mesh):
    return jax.shard_map(
        body,
        mesh=mesh,
        in_specs=(P(None, ("groups", "tm")), P(), P()),
        out_specs=(P(None, ("groups", "tm")), P(("groups", "tm"), None, None), P("groups")),
        check_vma=False,
    )
```

```python
import math

import jax
import jax.numpy as jnp
from jax import lax
from jax.experimental import pallas as pl
from jax.experimental.pallas import tpu as pltpu
from jax.sharding import PartitionSpec as P

ATOMS = 256
CHANNELS = 64
ATOM_LEN = 128
SPARSITY = 0.05
DICT_RATE = 0.5
EPSILON = 1e-06

SCALE = 1.0 / math.sqrt(CHANNELS * ATOM_LEN)
FINE = 16
COARSE = ATOM_LEN // FINE
WIDE = FINE * CHANNELS
HALO = 2 * ATOM_LEN
F32 = jnp.float32
BF16 = jnp.bfloat16
PITCH = CHANNELS + 8
CHUNKS = 2
PEERS = 8
OWN_LIMIT = 53 * 1024 * 1024
VMEM_LIMIT = 36 * 1024 * 1024


def vmem():
    return pl.BlockSpec(memory_space=pltpu.VMEM)


def smem():
    return pl.BlockSpec(memory_space=pltpu.SMEM)


def anywhere():
    return pl.BlockSpec(memory_space=pl.ANY)


def fetch_lags(source, lags, arrived):
    copies = [
        pltpu.make_async_copy(
            source.at[pl.ds(coarse * WIDE, WIDE), :],
            lags.at[pl.ds(coarse * WIDE, WIDE), :],
            arrived.at[coarse],
        )
        for coarse in range(COARSE)
    ]
    for copy in copies:
        copy.start()
    return copies


def cost(flops, bytes_accessed):
    return pl.CostEstimate(flops=flops, bytes_accessed=bytes_accessed, transcendentals=0)


def kernel_params(limit=VMEM_LIMIT):
    return pltpu.CompilerParams(vmem_limit_bytes=limit)


def shifted(value, axis, steps):
    count = lax.axis_size(axis)
    leading, last = (max(0, -steps), min(count, count - steps))
    return lax.ppermute(value, axis, [(source, source + steps) for source in range(leading, last)])


def swapped(value, bit):
    count = lax.axis_size("tm")
    return lax.ppermute(value, "tm", [(i, i ^ bit) for i in range(count)])


def fill_windows(pairs, windows, rows):
    for step in range(FINE // 2):
        windows[0:rows, step * 128 : (step + 1) * 128] = pairs[
            2 * step : 2 * step + rows, :
        ].astype(BF16)


def adjoint(windows, lags, total, spans, copies=None):
    rows = sum(count for _, count in spans)
    for coarse in range(COARSE):
        if copies is not None:
            copies[coarse].wait()
        shift = coarse * FINE
        taken = [windows[start + shift : start + shift + count, :] for start, count in spans]
        part = jnp.dot(
            taken[0] if len(taken) == 1 else jnp.concatenate(taken, 0),
            lags[coarse * WIDE : (coarse + 1) * WIDE, :],
            preferred_element_type=F32,
        )
        if coarse == 0:
            total[0:rows, :] = part
        else:
            total[0:rows, :] += part


def windows_of(whole, pairs, windows):
    length = whole.shape[1]
    both = jnp.concatenate([whole, pltpu.roll(whole, length - 1, 1)], 0)
    pairs[0:length, :] = both.T
    fill_windows(pairs, windows, length - FINE)


def turn_dictionary(atoms, lags, by_atom, by_lag, copies):
    half = ATOMS // 2
    for part in range(2):
        copies[part].wait()
        for atom in range(half):
            by_atom[atom * PITCH : atom * PITCH + CHANNELS, :] = atoms[part * half + atom].astype(
                F32
            )
        for channel in range(CHANNELS):
            turned = by_atom[pl.ds(channel, half, stride=PITCH), :].T
            by_lag[pl.ds(channel, ATOM_LEN, stride=PITCH), :] = turned
        for lag in range(ATOM_LEN):
            lags[lag * CHANNELS : (lag + 1) * CHANNELS, part * half : (part + 1) * half] = by_lag[
                lag * PITCH : lag * PITCH + CHANNELS, :
            ].astype(BF16)


def own_kernel(
    middle, right_any, atoms_any, gradient, largest, lags_out,
    right, atoms, lags, by_atom, by_lag, pairs, windows, sems, atom_sems,
):
    width = middle.shape[1]
    half = ATOMS // 2
    loads = [
        pltpu.make_async_copy(
            atoms_any.at[pl.ds(part * half, half)],
            atoms.at[pl.ds(part * half, half)],
            atom_sems.at[part],
        )
        for part in range(2)
    ]
    loads[0].start()
    near = pltpu.make_async_copy(right_any.at[:, pl.ds(0, HALO)], right, sems.at[COARSE])
    near.start()
    loads[1].start()
    near.wait()
    whole = jnp.concatenate([middle[...], right[:, 0:ATOM_LEN]], 1)
    windows_of(-whole, pairs, windows)
    turn_dictionary(atoms, lags, by_atom, by_lag, loads)
    copies = fetch_lags(lags, lags_out, sems)
    for begin, end in row_chunks(width):
        adjoint(windows, lags, gradient.at[pl.ds(begin, end - begin), :], [(begin, end - begin)])
    own = jnp.abs(gradient[...]) * SCALE
    folded = jnp.max(own.reshape(width // 8, 8, ATOMS), 0)
    folded = jnp.maximum(folded[:, :128], folded[:, 128:])
    for peer in range(largest.shape[0]):
        largest[peer] = folded
    for copy in copies:
        copy.wait()


def border_kernel(
    left_any, middle, right_any, lags, gradient, left, right, pairs, windows, sems
):
    near = [
        pltpu.make_async_copy(
            left_any.at[:, pl.ds(left_any.shape[1] - HALO, HALO)], left, sems.at[COARSE]),
        pltpu.make_async_copy(right_any.at[:, pl.ds(0, HALO)], right, sems.at[COARSE + 1]),
    ]
    for copy in near:
        copy.start()
    for copy in near:
        copy.wait()
    whole = jnp.concatenate([left[...], middle[:, 0:ATOM_LEN], right[...]], 1)
    windows_of(-whole, pairs, windows)
    adjoint(windows, lags, gradient.at[pl.ds(0, HALO), :], [(0, HALO)])
    adjoint(windows, lags, gradient.at[pl.ds(HALO, ATOM_LEN), :], [(HALO + ATOM_LEN, ATOM_LEN)])


def row_chunks(rows):
    size = -(-rows // (CHUNKS * FINE)) * FINE
    return [(low, min(low + size, rows)) for low in range(0, rows, size)]


def forward(codes, lags, wide, spread, folded, start, rows):
    keep = rows - FINE
    weights = jnp.concatenate(
        [lags[coarse * WIDE : (coarse + 1) * WIDE, :] for coarse in range(COARSE)], 1
    )
    done = 0
    for begin, end in row_chunks(rows):
        for coarse in range(COARSE):
            low = start + begin - coarse * FINE
            wide[begin:end, coarse * ATOMS : (coarse + 1) * ATOMS] = codes[
                low : low + end - begin, :
            ]
        spread[begin:end, :] = lax.dot_general(
            wide[begin:end, :], weights, (((1,), (1,)), ((), ())), preferred_element_type=F32
        )
        until = keep + 2 if end == rows else end - FINE
        total = spread[FINE - 2 + done : FINE - 2 + until, 0:128]
        for step in range(1, FINE // 2):
            low = FINE - 2 - 2 * step
            total = total + spread[low + done : low + until, step * 128 : (step + 1) * 128]
        folded[done:until, :] = total
        done = until
    return folded[2 : keep + 2, 0:64] + folded[1 : keep + 1, 64:128]


def soft(moved, bound):
    return jnp.where(moved > 0, 1.0, -1.0) * jnp.maximum(jnp.abs(moved) - bound, 0.0)


def second_kernel(
    left_any, middle, right_any, lags, own_gradient, border, peak, step, valid, *rest
):
    outs, scratch, kept = rest[:-12], rest[-12:-1], rest[-1]
    signal, codes, codes_low, pairs, windows, wide, spread, folded = scratch[:8]
    left, right, sems = scratch[8:]
    near = [
        pltpu.make_async_copy(
            left_any.at[:, pl.ds(left_any.shape[1] - HALO, HALO)], left, sems.at[COARSE]),
        pltpu.make_async_copy(right_any.at[:, pl.ds(0, HALO)], right, sems.at[COARSE + 1]),
    ]
    for copy in near:
        copy.start()
    for copy in near:
        copy.wait()
    width = middle.shape[1]
    step_size = step[0]
    threshold = SPARSITY * jnp.max(peak[...])
    bound = step_size * threshold
    low, high = valid[0], valid[1]
    whole = jnp.concatenate([left[...], middle[...], right[...]], 1)
    signal[...] = whole.T

    def row(start, count):
        return lax.broadcasted_iota(jnp.int32, (count, 1), 0) + start

    for start, values in (
        (0, border[0:HALO, :]),
        (HALO, own_gradient[...]),
        (HALO + width, border[HALO:, :]),
    ):
        count = values.shape[0]
        moved = -step_size * (values * SCALE)
        updated = soft(moved, bound)
        if start == 0:
            updated = jnp.where(row(0, count) >= low, updated, 0.0)
        codes[start : start + count, :] = updated
        codes_low[start : start + count, :] = updated.astype(BF16)
    rows2 = width + 2 * ATOM_LEN
    model = forward(codes_low, lags, wide, spread, folded, ATOM_LEN - FINE, rows2 + FINE)
    resid = model * SCALE - signal[ATOM_LEN : ATOM_LEN + rows2, :]
    resid = jnp.where(row(ATOM_LEN, rows2) < high, resid, 0.0)
    pairs[0:rows2, 0:64] = resid
    pairs[0 : rows2 - 1, 64:128] = pairs[1:rows2, 0:64]
    fill_windows(pairs, windows, rows2 - FINE)
    rows3 = width + ATOM_LEN
    for begin, end in row_chunks(rows3):
        target = spread.at[pl.ds(begin, end - begin), 0:ATOMS]
        adjoint(windows, lags, target, [(begin, end - begin)])
    before = codes[ATOM_LEN : ATOM_LEN + rows3, :]
    moved = before - step_size * (spread[0:rows3, 0:ATOMS] * SCALE)
    updated = jnp.where(row(ATOM_LEN, rows3) >= low, soft(moved, bound), 0.0)
    codes[0:rows3, :] = updated
    codes_low[0:rows3, :] = updated.astype(BF16)
    turned = updated.T
    outs[0][...] = turned[:, ATOM_LEN:]
    sparse = jnp.sum(jnp.abs(codes[ATOM_LEN:rows3, :]))
    model = forward(codes_low, lags, wide, spread, folded, ATOM_LEN - FINE, width + FINE)
    resid = model * SCALE - signal[HALO : HALO + width, :]
    resid_low = resid.T.astype(BF16)
    ahead = turned.astype(BF16)
    loss = 0.5 * jnp.sum(resid * resid) + threshold * sparse
    if len(outs) == 1 + PEERS:
        atoms = ATOMS // PEERS
        whole_loss = jnp.full((16, ATOM_LEN), loss, F32)
        high_part = whole_loss.astype(BF16)
        rest_loss = whole_loss - high_part.astype(F32)
        middle_part = rest_loss.astype(BF16)
        low_part = (rest_loss - middle_part.astype(F32)).astype(BF16)
        lane = lax.broadcasted_iota(jnp.int32, (16, ATOM_LEN), 1)
        tail = jnp.where(
            lane == 0,
            high_part.astype(F32),
            jnp.where(lane == 1, middle_part.astype(F32), low_part.astype(F32)),
        ).astype(BF16)
        kept[...] = ahead
        for turn in range(PEERS):
            first = pl.multiple_of(valid[2 + turn] * atoms, atoms)
            piece = outs[1 + turn]
            piece[0:atoms, :] = kept[pl.ds(first, atoms), ATOM_LEN:]
            piece[atoms : atoms + CHANNELS, :] = resid_low
            for part in range(atoms // 16):
                piece[atoms + CHANNELS :, part * ATOM_LEN : (part + 1) * ATOM_LEN] = kept[
                    pl.ds(pl.multiple_of(first + part * 16, 16), 16), 0:ATOM_LEN
                ]
            piece[atoms + CHANNELS :, HALO : HALO + ATOM_LEN] = tail
            piece[atoms + CHANNELS :, HALO + ATOM_LEN :] = jnp.zeros(
                (16, width - HALO - ATOM_LEN), BF16
            )
    else:
        outs[1][...] = ahead
        outs[2][...] = resid_low
        outs[3][...] = jnp.full((8, 128), loss, F32)


def correlate(codes_of, resid_of, blocks, atoms, width, stack, pairs, windows):
    main = blocks * width
    length = width + ATOM_LEN
    lane = lax.broadcasted_iota(jnp.int32, (atoms, ATOM_LEN), 1)
    extra = [jnp.zeros((atoms, ATOM_LEN), F32) for _ in range(COARSE)]
    windows[main : main + ATOM_LEN, :] = jnp.zeros((ATOM_LEN, WIDE), BF16)
    sums = None
    for block in range(blocks):
        piece = jnp.concatenate(
            [resid_of(block).astype(F32), jnp.zeros((CHANNELS, ATOM_LEN), F32)], 1
        )
        piece = pltpu.roll(piece, FINE, 1)
        both = jnp.concatenate([piece, pltpu.roll(piece, length - 1, 1)], 0)
        slot = pairs.at[block % 2]
        slot[...] = both.T
        for step in range(FINE // 2):
            lanes = slice(step * 128, (step + 1) * 128)
            low = 2 * step
            windows[main + block * FINE : main + (block + 1) * FINE, lanes] = slot[
                low : low + FINE, :
            ].astype(BF16)
            low += FINE
            windows[block * width : (block + 1) * width, lanes] = slot[
                low : low + width, :
            ].astype(BF16)
        held = codes_of(block).astype(F32)
        for coarse in range(COARSE):
            start = ATOM_LEN - coarse * FINE
            turned = pltpu.roll(held, length - start, 1)
            stack[coarse * atoms : (coarse + 1) * atoms, block * width : (block + 1) * width] = (
                turned[:, :width].astype(BF16)
            )
            turned = pltpu.roll(held, (FINE * block - (start - FINE)) % length, 1)[:, :ATOM_LEN]
            inside = (lane >= FINE * block) & (lane < FINE * (block + 1))
            extra[coarse] = jnp.where(inside, turned, extra[coarse])
        begin, end = block * width, (block + 1) * width
        part = jnp.dot(stack[:, begin:end], windows[begin:end, :], preferred_element_type=F32)
        sums = part if sums is None else sums + part
    for coarse in range(COARSE):
        stack[coarse * atoms : (coarse + 1) * atoms, main : main + ATOM_LEN] = extra[coarse].astype(
            BF16
        )
    return sums + jnp.dot(
        stack[:, main : main + ATOM_LEN],
        windows[main : main + ATOM_LEN, :],
        preferred_element_type=F32,
    )


def shared_part(pieces, stack, pairs, windows):
    rows, width = pieces[0].shape
    atoms = rows - CHANNELS - 16

    def codes_of(block):
        before = [
            pieces[block][atoms + CHANNELS :, part * ATOM_LEN : (part + 1) * ATOM_LEN]
            for part in range(atoms // 16)
        ]
        return jnp.concatenate(
            [jnp.concatenate(before, 0).astype(F32), pieces[block][0:atoms, :].astype(F32)], 1
        )

    def resid_of(block):
        return pieces[block][atoms : atoms + CHANNELS, :]

    loss = jnp.zeros((16, ATOM_LEN), F32)
    for piece in pieces:
        loss += piece[atoms + CHANNELS :, HALO : HALO + ATOM_LEN].astype(F32)
    lane = lax.broadcasted_iota(jnp.int32, (16, ATOM_LEN), 1)
    loss = jnp.sum(jnp.where(lane < 3, loss, 0.0), 1, keepdims=True)[0:8]
    total = correlate(
        codes_of, resid_of, len(pieces), atoms, width, stack, pairs, windows
    )
    return total, jnp.broadcast_to(loss, (8, WIDE))


def shared_first(*refs):
    pieces, (out, stack, pairs, windows) = refs[: PEERS // 2], refs[PEERS // 2 :]
    total, loss = shared_part(pieces, stack, pairs, windows)
    rows = total.shape[0]
    out[0:rows, :] = total
    out[rows:, :] = loss


def shared_second(core, before, *refs):
    pieces, (keep, give, stack, pairs, windows, total) = refs[: PEERS // 2], refs[PEERS // 2 :]
    sums, loss = shared_part(pieces, stack, pairs, windows)
    rows = total.shape[0]
    atoms = rows // COARSE
    total[...] = sums + before[0:rows, :]
    half = atoms // 2
    mine = core[0] * half
    other = half - mine
    for coarse in range(COARSE):
        rows_of = slice(coarse * half, (coarse + 1) * half)
        keep[rows_of, :] = total[pl.ds(coarse * atoms + mine, half), :]
        give[rows_of, :] = total[pl.ds(coarse * atoms + other, half), :]
    ending = loss + before[rows:, :]
    keep[COARSE * half :, :] = ending
    give[COARSE * half :, :] = ending


def lone_kernel(codes, resid, out, stack, pairs, windows):
    out[...] = correlate(
        lambda b: codes[...], lambda b: resid[...], 1, ATOMS, resid.shape[1], stack, pairs, windows
    )


def last_kernel(inverse, keep, recv_any, atoms_ref, out, loss_out, total, turned, recv, sem):
    copy = pltpu.make_async_copy(recv_any, recv, sem.at[0])
    copy.start()
    copy.wait()
    half = atoms_ref.shape[0]
    loss_out[0] = (keep[COARSE * half, 0] + recv[COARSE * half, 0]) * inverse
    for step in range(FINE // 2):
        lanes = slice(step * 128, (step + 1) * 128)
        total[step] = keep[0 : COARSE * half, lanes] + recv[0 : COARSE * half, lanes]
    for pair in range(half // 2):
        for step in range(FINE // 2):
            one = total.at[step][pl.ds(2 * pair, COARSE, stride=half), :]
            two = total.at[step][pl.ds(2 * pair + 1, COARSE, stride=half), :]
            block = turned.at[pair]
            block[pl.ds(2 * step, COARSE, stride=FINE), :] = jnp.concatenate(
                [one[:, 0:64], two[:, 0:64]], 1
            )
            block[pl.ds(2 * step + 1, COARSE, stride=FINE), :] = jnp.concatenate(
                [one[:, 64:128], two[:, 64:128]], 1
            )
    gradient = jnp.concatenate([turned[pair].T for pair in range(half // 2)], 0)
    gradient = gradient.reshape(half, CHANNELS, ATOM_LEN)
    normed = gradient / jnp.sqrt(
        jnp.mean(gradient * gradient, axis=(1, 2), keepdims=True) + EPSILON
    )
    moved = atoms_ref[...].astype(F32) - DICT_RATE * normed
    out[...] = moved / jnp.sqrt(jnp.mean(moved * moved, axis=(1, 2), keepdims=True) + EPSILON)


def body(signal, dictionary, step):
    width = signal.shape[1]
    count = lax.axis_size("tm")
    me = lax.axis_index("tm")
    left = shifted(signal, "tm", 1)
    right = shifted(signal, "tm", -1)
    rows1 = width + 3 * ATOM_LEN
    span = width + 2 * HALO

    near_scratch = [pltpu.VMEM((CHANNELS, HALO), F32)]
    sems = [pltpu.SemaphoreType.DMA((COARSE + 2,))]
    bordered = width + ATOM_LEN
    gradient, peak, lags = pl.pallas_call(
        own_kernel,
        out_shape=(
            jax.ShapeDtypeStruct((width, ATOMS), F32),
            jax.ShapeDtypeStruct((count, 8, 128), F32),
            jax.ShapeDtypeStruct((ATOM_LEN * CHANNELS, ATOMS), BF16),
        ),
        in_specs=[vmem(), anywhere(), pl.BlockSpec(memory_space=pltpu.HBM)],
        out_specs=(vmem(), vmem(), pl.BlockSpec(memory_space=pltpu.HBM)),
        scratch_shapes=near_scratch
        + [pltpu.VMEM(dictionary.shape, BF16)]
        + [pltpu.VMEM((ATOM_LEN * CHANNELS, ATOMS), BF16)]
        + [pltpu.VMEM((ATOM_LEN * PITCH, 128), F32)] * 2
        + [pltpu.VMEM((bordered, 128), F32), pltpu.VMEM((bordered, WIDE), BF16)]
        + sems
        + [pltpu.SemaphoreType.DMA((2,))],
        compiler_params=kernel_params(OWN_LIMIT),
        cost_estimate=cost(2 * width * ATOMS * WIDE * COARSE, 5 << 20),
    )(signal, right, dictionary)
    peak = lax.all_to_all(peak, "tm", 0, 0, tiled=False)
    span_border = 2 * HALO + ATOM_LEN
    border = pl.pallas_call(
        border_kernel,
        out_shape=jax.ShapeDtypeStruct((HALO + ATOM_LEN, ATOMS), F32),
        in_specs=[anywhere(), vmem(), anywhere(), vmem()],
        out_specs=vmem(),
        scratch_shapes=near_scratch * 2
        + [pltpu.VMEM((span_border, 128), F32), pltpu.VMEM((span_border, WIDE), BF16)]
        + sems,
        compiler_params=kernel_params(),
        cost_estimate=cost(2 * (HALO + ATOM_LEN) * ATOMS * WIDE * COARSE, 5 << 20),
    )(left, signal, right, lags)

    valid = jnp.stack(
        [jnp.where(me == 0, HALO, 0), jnp.where(me == count - 1, HALO + width, span)]
        + [(me // 2) ^ turn for turn in range(PEERS)]
    ).astype(jnp.int32)
    owned = ATOMS // count
    shared = count == 2 * PEERS
    own_atoms = lax.dynamic_slice_in_dim(dictionary, me * owned, owned, 0)
    if shared:
        rows = ATOMS // PEERS + CHANNELS + 16
        outs = (jax.ShapeDtypeStruct((rows, width), BF16),) * PEERS
    else:
        outs = (
            jax.ShapeDtypeStruct((ATOMS, width + ATOM_LEN), BF16),
            jax.ShapeDtypeStruct((CHANNELS, width), BF16),
            jax.ShapeDtypeStruct((8, 128), F32),
        )
    codes, *others = pl.pallas_call(
        second_kernel,
        out_shape=(jax.ShapeDtypeStruct((ATOMS, width), F32),) + outs,
        in_specs=[anywhere(), vmem(), anywhere(), vmem()] + [vmem()] * 3 + [smem()] * 2,
        out_specs=(vmem(),) * (1 + len(outs)),
        scratch_shapes=[
            pltpu.VMEM((span, CHANNELS), F32),
            pltpu.VMEM((rows1, ATOMS), F32),
            pltpu.VMEM((rows1, ATOMS), BF16),
            pltpu.VMEM((rows1, 128), F32),
            pltpu.VMEM((rows1, WIDE), BF16),
            pltpu.VMEM((rows1, COARSE * ATOMS), BF16),
            pltpu.VMEM((rows1, WIDE), F32),
            pltpu.VMEM((rows1, 128), F32),
        ]
        + near_scratch * 2
        + sems
        + [pltpu.VMEM((ATOMS, width + ATOM_LEN), BF16)],
        compiler_params=kernel_params(),
    )(left, signal, right, lags, gradient, border, peak, step, valid)

    def correlate_scratch(blocks, atoms):
        return [
            pltpu.VMEM((COARSE * atoms, blocks * width + ATOM_LEN), BF16),
            pltpu.VMEM((2, width + ATOM_LEN, 128), F32),
            pltpu.VMEM((blocks * width + ATOM_LEN, WIDE), BF16),
        ]

    inverse = 1.0 / (CHANNELS * width * count)
    if shared:
        core = me % 2
        pieces = list(others)
        for turn in range(1, PEERS):
            pieces[turn] = swapped(pieces[turn], 2 * turn)
        half_rows = jax.ShapeDtypeStruct((COARSE * owned + 8, WIDE), F32)
        blocks = PEERS // 2
        before = pl.pallas_call(
            shared_first,
            out_shape=jax.ShapeDtypeStruct((COARSE * 2 * owned + 8, WIDE), F32),
            in_specs=[vmem()] * blocks,
            out_specs=vmem(),
            scratch_shapes=correlate_scratch(blocks, 2 * owned),
            compiler_params=kernel_params(),
            cost_estimate=cost(2 * COARSE * 2 * owned * blocks * width * WIDE, 2 << 20),
        )(*[pieces[turn] for turn in (0, 4, 5, 6)])
        keep, give = pl.pallas_call(
            shared_second,
            out_shape=(half_rows, half_rows),
            in_specs=[smem(), vmem()] + [vmem()] * blocks,
            out_specs=(vmem(), vmem()),
            scratch_shapes=correlate_scratch(blocks, 2 * owned)
            + [pltpu.VMEM((COARSE * 2 * owned, WIDE), F32)],
            compiler_params=kernel_params(),
            cost_estimate=cost(2 * COARSE * 2 * owned * blocks * width * WIDE, 2 << 20),
        )(core.reshape(1).astype(jnp.int32), before, *[pieces[turn] for turn in (7, 3, 2, 1)])
        recv = swapped(give, 1)
        new_dictionary, loss = pl.pallas_call(
            lambda *refs: last_kernel(inverse, *refs),
            out_shape=(
                jax.ShapeDtypeStruct((owned, CHANNELS, ATOM_LEN), F32),
                jax.ShapeDtypeStruct((1,), F32),
            ),
            in_specs=[vmem(), anywhere(), vmem()],
            out_specs=(vmem(), smem()),
            scratch_shapes=[
                pltpu.VMEM((FINE // 2, COARSE * owned, 128), F32),
                pltpu.VMEM((owned // 2, ATOM_LEN, 2 * CHANNELS), F32),
                pltpu.VMEM(half_rows.shape, F32),
                pltpu.SemaphoreType.DMA((1,)),
            ],
            compiler_params=kernel_params(),
        )(keep, recv, own_atoms)
        return (codes, new_dictionary, loss)

    ahead, resid, loss = others
    part = pl.pallas_call(
        lone_kernel,
        out_shape=jax.ShapeDtypeStruct((COARSE * ATOMS, WIDE), F32),
        in_specs=[vmem()] * 2,
        out_specs=vmem(),
        scratch_shapes=correlate_scratch(1, ATOMS),
        compiler_params=kernel_params(),
    )(ahead, resid)
    summed = lax.psum_scatter(
        part.reshape(COARSE, ATOMS, WIDE), "tm", scatter_dimension=1, tiled=True
    )
    atom_gradient = (
        summed.reshape(COARSE, owned, FINE, CHANNELS)
        .transpose(1, 3, 0, 2)
        .reshape(owned, CHANNELS, ATOM_LEN)
    )
    normed = atom_gradient / jnp.sqrt(
        jnp.mean(atom_gradient * atom_gradient, axis=(1, 2), keepdims=True) + EPSILON
    )
    moved = own_atoms.astype(F32) - DICT_RATE * normed
    new_dictionary = moved / jnp.sqrt(
        jnp.mean(moved * moved, axis=(1, 2), keepdims=True) + EPSILON
    )
    bit = 1
    while bit < count:
        loss = loss + swapped(loss, bit)
        bit *= 2
    return (codes, new_dictionary, loss[0, :1] * inverse)


def solution(mesh):
    return jax.shard_map(
        body,
        mesh=mesh,
        in_specs=(P(None, ("groups", "tm")), P(), P()),
        out_specs=(P(None, ("groups", "tm")), P(("groups", "tm"), None, None), P("groups")),
        check_vma=False,
    )
```
